256 devices in a mesh: seq: 16 (over z, core), dp: 16 (over x, y).
Axes of the slice: x: 4, y: 4, z: 8, core: 2. Of those that a mesh axis runs over, the one named last changes fastest.
Arguments:
- q_proj: bfloat16 [16, 3072, 16, 128], P('dp', 'seq'), may hold values from -6 to 6
- k_proj: bfloat16 [16, 3072, 4, 128], P('dp', 'seq'), may hold values from -6 to 6
- v_proj: bfloat16 [16, 3072, 4, 128], P('dp', 'seq'), may hold values from -6 to 6
- upstream: bfloat16 [16, 3072, 16, 128], P('dp', 'seq'), may hold values from -6 to 6
- segment_ids: int32 [16, 3072], P('dp', 'seq'), may hold values from 0 to 6, as said below
- tree_tiles: int32 [16, 140, 3], P('dp'), may hold values from 0 to 23, as said below
- rewards: float32 [16, 5], P('dp'), may hold values from 0 to 1
- q_gain: float32 [128], replicated, may hold values from 0.1 to 1.9
- k_gain: float32 [128], replicated, may hold values from 0.1 to 1.9
Outputs:
- attn_out: bfloat16 [16, 3072, 16, 128], P('dp', 'seq')
- dq_proj: bfloat16 [16, 3072, 16, 128], P('dp', 'seq')
- dk_proj: bfloat16 [16, 3072, 4, 128], P('dp', 'seq')
- dv_proj: bfloat16 [16, 3072, 4, 128], P('dp', 'seq')
- q_gain_grad: float32 [128], replicated
- k_gain_grad: float32 [128], replicated
The draws below stay inside these ranges and needn't reach their ends.
Inputs may be any that keep to these rules, and one draw needn't show every extreme that they name: `tree_tiles`: kind 0 entries are padding. Each response fills 1 to 4 whole tiles right after the prompt or the previous response; its tokens see all prompt tiles fully, earlier tiles of the same response fully and their own tile by kind 2; the prompt's 4 tiles see each other causally. Live entries are distinct and in no fixed order. `segment_ids`: agrees with tree_tiles: segments follow the tile order of the tree; empty slots come last.
All inputs are finite; a program needn't handle non-finite values.
Results may differ from the reference program's by a relative error of at most 0.012.
Values may be sent and summed in bfloat16 or wider, within the bound.
No kernel may reach another device: no remote copies, remote signals or barrier semaphores. Data moves between devices by JAX's collectives and lax.ppermute only.
A program may use at most 128 MiB of HBM per device.

```python
import math
import jax
import jax.numpy as jnp
from jax import lax

HEADS = 16
KV_HEADS = 4
HEAD_DIM = 128
BLOCK = 128
RESPONSES = 5
SEQ_TOKENS = 3072
GROUPS = 16
MAX_TILES = 140


def response_blocks(key):
    count_key, full_key = jax.random.split(key)
    counts = jax.random.randint(count_key, (GROUPS, RESPONSES), 1, 5)
    chosen = jax.random.randint(full_key, (), 0, GROUPS)
    return jnp.where(jnp.arange(GROUPS)[:, None] == chosen, 4, counts).astype(jnp.int32)


def block_segments(counts):
    block_count = SEQ_TOKENS // BLOCK
    ends = 4 + jnp.cumsum(counts, axis=1)
    starts = ends - counts
    tile_ids = jnp.arange(block_count, dtype=jnp.int32)
    segment = jnp.sum((tile_ids[None, :, None] >= starts[:, None, :]).astype(jnp.int32), axis=2)
    filled = tile_ids[None, :] < ends[:, -1:]
    return jnp.where(filled, segment, RESPONSES + 1).astype(jnp.int32)


def draw_segment_ids(key, part):
    counts = response_blocks(key)
    return jnp.repeat(block_segments(counts), BLOCK, axis=1)


def draw_tree_tiles(key, part):
    counts = response_blocks(key)
    key = jax.random.fold_in(key, 7)
    block_count = SEQ_TOKENS // BLOCK
    segs = block_segments(counts)
    query_seg = segs[:, :, None]
    key_seg = segs[:, None, :]
    query_tile = jnp.arange(block_count, dtype=jnp.int32)[None, :, None]
    key_tile = jnp.arange(block_count, dtype=jnp.int32)[None, None, :]
    causal = jnp.where(key_tile == query_tile, 2, jnp.where(key_tile < query_tile, 1, 0))
    prompt_kind = jnp.where(key_tile < 4, causal, 0)
    same_tree = (query_seg == key_seg) | (key_tile < 4)
    answer_kind = jnp.where((query_seg <= RESPONSES) & same_tree, causal, 0)
    kinds = jnp.where(query_tile < 4, prompt_kind, answer_kind).astype(jnp.int32)
    flat = kinds.reshape(GROUPS, block_count * block_count)
    flat_ids = jnp.arange(block_count * block_count, dtype=jnp.int32)[None, :]
    order_key = jnp.where(flat > 0, flat_ids, block_count * block_count + flat_ids)
    picked = jnp.argsort(order_key, axis=1, stable=True)[:, :MAX_TILES].astype(jnp.int32)
    picked_kind = jnp.take_along_axis(flat, picked, axis=1)
    alive = picked_kind > 0
    query_part = jnp.where(alive, picked // block_count, 0)
    key_part = jnp.where(alive, picked % block_count, 0)
    shuffle_scores = jax.random.randint(key, (GROUPS, MAX_TILES), 0, 1048576) * MAX_TILES + jnp.arange(MAX_TILES, dtype=jnp.int32)[None, :]
    shuffle = jnp.argsort(shuffle_scores, axis=1, stable=True).astype(jnp.int32)
    stacked = jnp.stack([query_part, key_part, picked_kind], axis=2)
    return jnp.take_along_axis(stacked, shuffle[:, :, None], axis=1).astype(jnp.int32)


def block_scale(own_key, extent, cuts, least, top_value):
    factor_of, own = 1.0, jax.random.fold_in(own_key, 6)
    for axis_at, blocks in cuts:
        heights = jnp.exp(jax.random.uniform(jax.random.fold_in(own, axis_at), (blocks,), jnp.float32, least / len(cuts), top_value / len(cuts)))
        factor_of = factor_of * jnp.repeat(heights, extent[axis_at] // blocks).reshape([-1 if axis == axis_at else 1 for axis in range(len(extent))])
    return factor_of


def normal_values(own_key, dims, deviation, reach, cuts=(), held_as=jnp.bfloat16):
    loudness = block_scale(own_key, dims, cuts, -0.22, 0.18) if cuts else 1.0
    drawn = jax.random.normal(own_key, dims, jnp.float32) * deviation * loudness
    return jnp.minimum(jnp.maximum(drawn, -reach), reach).astype(held_as)


def setup_inputs(seed: int = 0) -> dict:
    seeds = jax.random.split(jax.random.key(seed), 10)
    q_proj = normal_values(seeds[0], (GROUPS, SEQ_TOKENS, HEADS, HEAD_DIM), 1.0, 6.0, ((0, 16), (1, 16)))
    k_proj = normal_values(seeds[1], (GROUPS, SEQ_TOKENS, KV_HEADS, HEAD_DIM), 1.0, 6.0, ((0, 16), (1, 16)))
    v_proj = normal_values(seeds[2], (GROUPS, SEQ_TOKENS, KV_HEADS, HEAD_DIM), 1.0, 6.0, ((0, 16), (1, 16)))
    upstream = normal_values(seeds[3], (GROUPS, SEQ_TOKENS, HEADS, HEAD_DIM), 1.0, 6.0, ((0, 16), (1, 16)))
    segment_ids = draw_segment_ids(jax.random.fold_in(seeds[9], 71), 0)
    tree_tiles = draw_tree_tiles(jax.random.fold_in(seeds[9], 71), 0)
    rewards = jnp.clip(1.0 * jax.random.uniform(seeds[6], (GROUPS, RESPONSES), jnp.float32) ** block_scale(seeds[6], (GROUPS, RESPONSES), ((0, 16),), -0.2, 0.2), 0.0, 1.0)
    q_gain = jnp.clip(1.0 + 0.18 * jax.random.normal(seeds[7], (HEAD_DIM,), jnp.float32), 0.1, 1.9)
    k_gain = jnp.clip(1.0 + 0.18 * jax.random.normal(seeds[8], (HEAD_DIM,), jnp.float32), 0.1, 1.9)
    return {"q_proj": q_proj, "k_proj": k_proj, "v_proj": v_proj, "upstream": upstream, "segment_ids": segment_ids, "tree_tiles": tree_tiles, "rewards": rewards, "q_gain": q_gain, "k_gain": k_gain}


norm_eps = 1e-06
rope_base = 1000000.0

def tree_table(tile_list, block_count):
    query_tile = tile_list[:, 0]
    key_tile = tile_list[:, 1]
    tile_kind = tile_list[:, 2]
    tile_ids = jnp.arange(block_count, dtype=jnp.int32)
    row_hits = (query_tile[:, None] == tile_ids[None, :]).astype(jnp.int32) * tile_kind[:, None]
    col_hits = (key_tile[:, None] == tile_ids[None, :]).astype(jnp.int32)
    table = jnp.einsum('tq,tk->qk', row_hits, col_hits)
    candidate = jnp.where((table > 0) & (tile_ids[None, :] >= 4), tile_ids[None, :], block_count)
    return (table, lax.optimization_barrier(jnp.min(candidate, axis=1)))

def positions(token_at, first_tile, block_count):
    tile_of = token_at // BLOCK
    tile_ids = jnp.arange(block_count, dtype=jnp.int32)
    begins = lax.optimization_barrier(jnp.sum((tile_of[:, None] == tile_ids[None, :]).astype(jnp.int32) * first_tile[None, :], axis=1))
    inside = (tile_of >= 4) & (begins < block_count)
    return jnp.where(inside, 4 * BLOCK + token_at - begins * BLOCK, token_at)

def rope_tables(place, head_width):
    half_width = head_width // 2
    freq = jnp.exp(jnp.arange(half_width, dtype=jnp.float32) * (-2.0 * math.log(rope_base) / head_width))
    angle = place.astype(jnp.float32)[:, None] * freq[None, :]
    cosine = jnp.cos(angle)
    sine = jnp.sin(angle)
    return (jnp.concatenate([cosine, cosine], axis=1), jnp.concatenate([sine, sine], axis=1))

def prepare(values, gain, cosine, sine):
    factor = lax.rsqrt(lax.optimization_barrier(jnp.mean(values * values, axis=-1, keepdims=True)) + norm_eps)
    normed = values * factor * gain
    half_width = normed.shape[-1] // 2
    turned = jnp.concatenate([-normed[..., half_width:], normed[..., :half_width]], axis=-1)
    return normed * cosine[:, None, :] + turned * sine[:, None, :]

def block_mask(table, row_start, key_begin):
    upper = table[row_start // BLOCK:row_start // BLOCK + 4]
    kinds = jnp.concatenate([upper[:, :4], upper[:, key_begin // BLOCK:key_begin // BLOCK + 7]], axis=1)
    kinds = jnp.repeat(jnp.repeat(kinds, BLOCK, axis=0), BLOCK, axis=1)
    query_at = row_start + jnp.arange(4 * BLOCK, dtype=jnp.int32)
    key_at = jnp.concatenate([jnp.arange(4 * BLOCK, dtype=jnp.int32), key_begin + jnp.arange(7 * BLOCK, dtype=jnp.int32)])
    return (kinds == 1) | (kinds == 2) & (key_at[None, :] <= query_at[:, None])

def block_step(query_rows, key_rows, value_rows, grad_rows, allowed, factor):
    scores = jnp.dot(query_rows, key_rows.T, preferred_element_type=jnp.float32) * factor
    unnormed = jnp.where(allowed, jnp.exp(scores), 0.0)
    totals = lax.optimization_barrier(jnp.sum(unnormed, axis=1, keepdims=True))
    weights = (unnormed / jnp.where(totals > 0, totals, 1.0)).astype(jnp.bfloat16)
    out_rows = jnp.dot(weights, value_rows, preferred_element_type=jnp.float32).astype(jnp.bfloat16)
    dweights = jnp.dot(grad_rows, value_rows.T, preferred_element_type=jnp.float32)
    weights_wide = weights.astype(jnp.float32)
    deltas = lax.optimization_barrier(jnp.sum(weights_wide * dweights, axis=1, keepdims=True))
    dscores = (weights_wide * (dweights - deltas) * factor).astype(jnp.bfloat16)
    dq_rows = jnp.dot(dscores, key_rows, preferred_element_type=jnp.float32).astype(jnp.bfloat16)
    dk_rows = jnp.dot(dscores.T, query_rows, preferred_element_type=jnp.float32)
    dv_rows = jnp.dot(weights.T, grad_rows, preferred_element_type=jnp.float32)
    return (out_rows, dq_rows, dk_rows, dv_rows)

def head_attention(query_head, key_head, value_head, grad_head, table):
    seq_len, head_width = query_head.shape
    factor = 1.0 / math.sqrt(head_width)
    prompt_len = 4 * BLOCK
    window = 7 * BLOCK
    out_parts = []
    dq_parts = []
    dk_total = jnp.zeros((seq_len, head_width), jnp.float32)
    dv_total = jnp.zeros((seq_len, head_width), jnp.float32)
    for row_start in range(0, seq_len, 4 * BLOCK):
        key_begin = min(max(row_start - 3 * BLOCK, prompt_len), seq_len - window)
        key_rows = jnp.concatenate([key_head[:prompt_len], key_head[key_begin:key_begin + window]], axis=0)
        value_rows = jnp.concatenate([value_head[:prompt_len], value_head[key_begin:key_begin + window]], axis=0)
        allowed = block_mask(table, row_start, key_begin)
        out_rows, dq_rows, dk_rows, dv_rows = block_step(query_head[row_start:row_start + 4 * BLOCK], key_rows, value_rows, grad_head[row_start:row_start + 4 * BLOCK], allowed, factor)
        out_parts.append(out_rows)
        dq_parts.append(dq_rows)
        dk_total = dk_total.at[:prompt_len].add(dk_rows[:prompt_len]).at[key_begin:key_begin + window].add(dk_rows[prompt_len:])
        dv_total = dv_total.at[:prompt_len].add(dv_rows[:prompt_len]).at[key_begin:key_begin + window].add(dv_rows[prompt_len:])
    return (jnp.concatenate(out_parts, axis=0), jnp.concatenate(dq_parts, axis=0), dk_total, dv_total)

def group_pass(q_proj, k_proj, v_proj, upstream, segment_ids, tree_tiles, rewards, q_gain, k_gain):
    seq_len, head_count, head_width = q_proj.shape
    kv_count = k_proj.shape[1]
    group_size = head_count // kv_count
    block_count = seq_len // BLOCK
    table, first_tile = tree_table(tree_tiles, block_count)
    place = positions(jnp.arange(seq_len, dtype=jnp.int32), first_tile, block_count)
    cosine, sine = rope_tables(place, head_width)

    def rotate(values, gain):
        return prepare(values, gain, cosine, sine)
    q_turned, q_pull = jax.vjp(rotate, q_proj.astype(jnp.float32), q_gain)
    k_turned, k_pull = jax.vjp(rotate, k_proj.astype(jnp.float32), k_gain)
    q_rot = q_turned.astype(jnp.bfloat16)
    k_rot = k_turned.astype(jnp.bfloat16)
    advantage = rewards - jnp.mean(rewards)
    labels = jnp.arange(1, RESPONSES + 1, dtype=jnp.int32)
    token_adv = lax.optimization_barrier(jnp.sum(jnp.where(segment_ids[:, None] == labels[None, :], advantage[None, :], 0.0), axis=1))
    grad_out = (upstream.astype(jnp.float32) * token_adv[:, None, None]).astype(jnp.bfloat16)

    def per_kv(items):
        query_group, key_one, value_one, grad_group = items
        outs_list = []
        dq_list = []
        dk_sum = jnp.zeros((seq_len, head_width), jnp.float32)
        dv_sum = jnp.zeros((seq_len, head_width), jnp.float32)
        for member in range(group_size):
            out_head, dq_head, dk_head, dv_head = head_attention(query_group[:, member], key_one, value_one, grad_group[:, member], table)
            outs_list.append(out_head)
            dq_list.append(dq_head)
            dk_sum = dk_sum + dk_head
            dv_sum = dv_sum + dv_head
        return (jnp.stack(outs_list, axis=1), jnp.stack(dq_list, axis=1), dk_sum, dv_sum)

    def grouped(values):
        return jnp.moveaxis(values.reshape(seq_len, kv_count, group_size, head_width), 1, 0)
    out_groups, dq_groups, dk_groups, dv_groups = lax.map(per_kv, (grouped(q_rot), jnp.moveaxis(k_rot, 1, 0), jnp.moveaxis(v_proj, 1, 0), grouped(grad_out)))
    attn_out = jnp.moveaxis(out_groups, 0, 1).reshape(seq_len, head_count, head_width)
    dq_rot = jnp.moveaxis(dq_groups, 0, 1).reshape(seq_len, head_count, head_width)
    dk_rot = jnp.moveaxis(dk_groups, 0, 1)
    dv_proj = jnp.moveaxis(dv_groups, 0, 1).astype(jnp.bfloat16)
    dq_in, dq_gain = q_pull(dq_rot.astype(jnp.float32))
    dk_in, dk_gain = k_pull(dk_rot)
    return (attn_out, dq_in.astype(jnp.bfloat16), dk_in.astype(jnp.bfloat16), dv_proj, dq_gain, dk_gain)

def reference(q_proj, k_proj, v_proj, upstream, segment_ids, tree_tiles, rewards, q_gain, k_gain):

    def one_group(items):
        return group_pass(items[0], items[1], items[2], items[3], items[4], items[5], items[6], q_gain, k_gain)
    results = lax.map(one_group, (q_proj, k_proj, v_proj, upstream, segment_ids, tree_tiles, rewards))
    return (results[0], results[1], results[2], results[3], lax.optimization_barrier(jnp.sum(results[4], axis=0)), lax.optimization_barrier(jnp.sum(results[5], axis=0)))
```

```python
import functools
import math

import jax
import jax.numpy as jnp
import numpy as np
from jax import lax
from jax.experimental import pallas as pl
from jax.experimental.pallas import tpu as pltpu
from jax.sharding import PartitionSpec as P

TILE = 128
PROMPT = 4
WINDOW = 5
SPAN = PROMPT + WINDOW
RESPONSES = 5
HEADS = 16
KV = 4
GROUP = HEADS // KV
WIDTH = 128
HALF = 64
EPS = 1e-06
ROPE_BASE = 1000000.0
F32 = jnp.float32
BF16 = jnp.bfloat16


def rope_tables(count):
    freq = np.exp(
        np.arange(WIDTH // 2, dtype=np.float32) * np.float32(-2.0 * math.log(ROPE_BASE) / WIDTH)
    ).astype(np.float32)
    angle = (np.arange(count, dtype=np.float32)[:, None] * freq[None, :]).astype(np.float64)
    cosine, sine = np.cos(angle), np.sin(angle)
    return (
        np.concatenate([cosine, cosine], axis=1).astype(np.float32),
        np.concatenate([-sine, sine], axis=1).astype(np.float32),
    )


def swap_halves(x):
    return pltpu.roll(x, WIDTH // 2, 1)


def mean_lanes(x):
    return jnp.sum(x, axis=1, keepdims=True) * (1.0 / WIDTH)


def rows_to_eight(x):
    return jnp.sum(x.reshape(-1, 8, WIDTH), axis=0)


def attention_kernel(
    blocks,
    tile_count,
    tiles_ref,
    rewards_ref,
    seg_ref,
    qgain_ref,
    kgain_ref,
    cos_ref,
    sin_ref,
    q_ref,
    up_ref,
    kv_hbm,
    out_ref,
    dq_ref,
    gains_ref,
    dkv_hbm,
    table,
    kvb,
    xkv,
    ykv,
    xq,
    xu,
    os_,
    dqs,
    kr,
    kt,
    vr,
    vt,
    dk,
    dv,
    ebuf,
    pbuf,
    qsum,
    ksum,
    zeros,
    in_sem,
    out_sem,
):
    me = lax.axis_index("seq")
    first_tile = (blocks * me) // 2
    wb = jnp.clip(first_tile - 3, PROMPT, tile_count - WINDOW)
    load_prompt = pltpu.make_async_copy(
        kv_hbm.at[pl.ds(0, PROMPT * TILE)], kvb.at[pl.ds(0, PROMPT * TILE)], in_sem.at[0]
    )
    load_window = pltpu.make_async_copy(
        kv_hbm.at[pl.ds(wb * TILE, WINDOW * TILE)],
        kvb.at[pl.ds(PROMPT * TILE, WINDOW * TILE)],
        in_sem.at[1],
    )
    load_prompt.start()
    load_window.start()

    zeros[...] = jnp.zeros_like(zeros)

    def zero_copy(tile):
        return pltpu.make_async_copy(
            zeros, dkv_hbm.at[pl.ds(tile * TILE, TILE)], out_sem.at[2 + tile]
        )

    for tile in range(PROMPT, tile_count):

        @pl.when((tile < wb) | (tile >= wb + WINDOW))
        def _(tile=tile):
            zero_copy(tile).start()

    def clear(at, carry):
        table[at] = 0
        return carry

    lax.fori_loop(0, tile_count * tile_count, clear, 0)

    def fill(at, carry):
        slot = tiles_ref[3 * at] * tile_count + tiles_ref[3 * at + 1]
        table[slot] = table[slot] + tiles_ref[3 * at + 2]
        return carry

    lax.fori_loop(0, tiles_ref.shape[0] // 3, fill, 0)

    def place_tile(a):
        def look(b, found):
            hit = table[a * tile_count + tile_count - 1 - b] > 0
            return jnp.where(hit, tile_count - 1 - b, found)

        found = lax.fori_loop(0, tile_count - PROMPT, look, tile_count)
        inside = (a >= PROMPT) & (found < tile_count)
        return jnp.minimum(jnp.where(inside, PROMPT + a - found, a), 2 * PROMPT - 1)

    key_place = [tile * TILE for tile in range(PROMPT)]
    key_place += [pl.multiple_of(place_tile(wb + j) * TILE, TILE) for j in range(WINDOW)]

    xq[...] = q_ref[...].astype(F32).reshape(xq.shape)
    xu[...] = up_ref[...].astype(F32).reshape(xu.shape)
    qgain = qgain_ref[...]
    kgain = kgain_ref[...]
    qsum[...] = jnp.zeros_like(qsum)
    ksum[...] = jnp.zeros_like(ksum)

    reward = [rewards_ref[r] for r in range(RESPONSES)]
    centre = (reward[0] + reward[1] + reward[2] + reward[3] + reward[4]) * (1.0 / RESPONSES)
    seg = seg_ref[...]
    adv_row = jnp.zeros(seg.shape, F32)
    for r in range(RESPONSES):
        adv_row = adv_row + jnp.where(seg == r + 1, reward[r] - centre, 0.0)

    load_prompt.wait()
    load_window.wait()

    def widen(tile, carry):
        rows = kvb[pl.ds(tile * TILE, TILE)].astype(F32).reshape(TILE * 2 * KV, WIDTH)
        xkv[pl.ds(pl.multiple_of(tile * TILE * 2 * KV, TILE * 2 * KV), TILE * 2 * KV), :] = rows
        return carry

    lax.fori_loop(0, SPAN, widen, 0)

    scale = 1.0 / math.sqrt(WIDTH)
    key_at = lax.broadcasted_iota(jnp.int32, (TILE, GROUP * HALF), 0)
    lane = lax.broadcasted_iota(jnp.int32, (1, GROUP * HALF), 1)

    def per_kv(g, carry):
        for tile in range(SPAN):
            x = xkv[pl.ds(tile * TILE * 2 * KV + g, TILE, stride=2 * KV), :]
            factor = lax.rsqrt(mean_lanes(x * x) + EPS)
            normed = x * factor * kgain
            cosine = cos_ref[pl.ds(key_place[tile], TILE), :]
            sine = sin_ref[pl.ds(key_place[tile], TILE), :]
            turned = normed * cosine + swap_halves(normed) * sine
            kr[tile] = turned.astype(BF16)
            kt[tile] = turned.T.astype(BF16)
            value = xkv[pl.ds(tile * TILE * 2 * KV + KV + g, TILE, stride=2 * KV), :]
            vr[tile] = value.astype(BF16)
            vt[tile] = value.T.astype(BF16)
        dk[...] = jnp.zeros_like(dk)
        dv[...] = jnp.zeros_like(dv)
        for i in range(blocks):
            block = blocks * me + i
            a = block // 2
            half = lax.rem(block, 2) * HALF
            off = jnp.maximum(a - 3 - wb, 0)
            starts = [0, 2, PROMPT + off, PROMPT + off + 2]
            names = [0, 2, wb + off, wb + off + 2]
            place = pl.multiple_of(place_tile(a) * TILE + half, HALF)
            cosine = jnp.concatenate([cos_ref[pl.ds(place, HALF), :]] * GROUP, axis=0)
            sine = jnp.concatenate([sin_ref[pl.ds(place, HALF), :]] * GROUP, axis=0)

            def rows(ref):
                return jnp.concatenate(
                    [
                        ref[pl.ds(i * HALF * HEADS + GROUP * g + h, HALF, stride=HEADS), :]
                        for h in range(GROUP)
                    ],
                    axis=0,
                )

            x = rows(xq)
            factor = lax.rsqrt(mean_lanes(x * x) + EPS)
            unit = x * factor
            normed = unit * qgain
            turned = normed * cosine + swap_halves(normed) * sine
            query = turned.astype(BF16)
            query_t = turned.T.astype(BF16)
            adv = jnp.concatenate([adv_row[:, i * HALF : (i + 1) * HALF]] * GROUP, axis=1)
            grad_f = rows(xu).T * adv
            grad_t = grad_f.astype(BF16)
            grad = grad_f.T.astype(BF16)

            slot = half + lax.rem(lane, HALF)
            total = jnp.zeros((1, GROUP * HALF), F32)
            for c in range(4):
                score = jnp.dot(
                    kr[pl.ds(starts[c], 2)].reshape(2 * TILE, WIDTH),
                    query_t,
                    preferred_element_type=F32,
                )
                for t in range(2):
                    kind = table[a * tile_count + names[c] + t]
                    one = (kind == 1).astype(jnp.int32)
                    two = (kind == 2).astype(jnp.int32)
                    limit = two * slot + (one * (TILE + 1) - 1 + two)
                    raw = jnp.where(
                        key_at <= limit,
                        jnp.exp2(score[t * TILE : (t + 1) * TILE] * (scale * math.log2(math.e))),
                        0.0,
                    )
                    ebuf[c, t * TILE : (t + 1) * TILE] = raw
                    total = total + jnp.sum(raw, axis=0, keepdims=True)
            share = jnp.where(total > 0, 1.0 / total, 0.0)
            out_t = jnp.zeros((WIDTH, GROUP * HALF), F32)
            for c in range(4):
                weights = (ebuf[c] * share).astype(BF16)
                pbuf[c] = weights
                value_t = jnp.concatenate([vt[starts[c]], vt[starts[c] + 1]], axis=1)
                out_t = out_t + jnp.dot(value_t, weights, preferred_element_type=F32)
            delta = jnp.sum(grad_t.astype(F32) * out_t, axis=0, keepdims=True)
            dq_t = jnp.zeros((WIDTH, GROUP * HALF), F32)
            for c in range(4):
                dweights = jnp.dot(
                    vr[pl.ds(starts[c], 2)].reshape(2 * TILE, WIDTH),
                    grad_t,
                    preferred_element_type=F32,
                )
                weights = pbuf[c]
                ds = (weights.astype(F32) * ((dweights - delta) * scale)).astype(BF16)
                key_t = jnp.concatenate([kt[starts[c]], kt[starts[c] + 1]], axis=1)
                dq_t = dq_t + jnp.dot(key_t, ds, preferred_element_type=F32)
                dk_c = jnp.dot(ds, query, preferred_element_type=F32)
                dv_c = jnp.dot(weights, grad, preferred_element_type=F32)
                dk[pl.ds(starts[c], 2)] += dk_c.reshape(2, TILE, WIDTH)
                dv[pl.ds(starts[c], 2)] += dv_c.reshape(2, TILE, WIDTH)

            dturned = dq_t.T.astype(BF16).astype(F32)
            dnormed = dturned * cosine - swap_halves(dturned) * sine
            qsum[...] += rows_to_eight(dnormed * unit)
            dunit = dnormed * qgain
            dx = factor * (dunit - unit * mean_lanes(dunit * unit))
            out = out_t.T
            for h in range(GROUP):
                spot = pl.ds(i * HALF * HEADS + GROUP * g + h, HALF, stride=HEADS)
                os_[spot, :] = out[h * HALF : (h + 1) * HALF]
                dqs[spot, :] = dx[h * HALF : (h + 1) * HALF]

        for tile in range(SPAN):
            x = xkv[pl.ds(tile * TILE * 2 * KV + g, TILE, stride=2 * KV), :]
            factor = lax.rsqrt(mean_lanes(x * x) + EPS)
            unit = x * factor
            cosine = cos_ref[pl.ds(key_place[tile], TILE), :]
            sine = sin_ref[pl.ds(key_place[tile], TILE), :]
            dturned = dk[tile]
            dnormed = dturned * cosine - swap_halves(dturned) * sine
            ksum[...] += rows_to_eight(dnormed * unit)
            dunit = dnormed * kgain
            dx = factor * (dunit - unit * mean_lanes(dunit * unit))
            ykv[pl.ds(tile * TILE * 2 * KV + g, TILE, stride=2 * KV), :] = dx
            ykv[pl.ds(tile * TILE * 2 * KV + KV + g, TILE, stride=2 * KV), :] = dv[tile]
        return carry

    lax.fori_loop(0, KV, per_kv, 0)

    def narrow(tile, carry):
        at = pl.multiple_of(tile * TILE * 2 * KV, TILE * 2 * KV)
        rows = ykv[pl.ds(at, TILE * 2 * KV), :]
        kvb[pl.ds(tile * TILE, TILE)] = rows.reshape(TILE, 2 * KV, WIDTH).astype(BF16)
        return carry

    lax.fori_loop(0, SPAN, narrow, 0)
    store_prompt = pltpu.make_async_copy(
        kvb.at[pl.ds(0, PROMPT * TILE)], dkv_hbm.at[pl.ds(0, PROMPT * TILE)], out_sem.at[0]
    )
    store_window = pltpu.make_async_copy(
        kvb.at[pl.ds(PROMPT * TILE, WINDOW * TILE)],
        dkv_hbm.at[pl.ds(wb * TILE, WINDOW * TILE)],
        out_sem.at[1],
    )
    store_prompt.start()
    store_window.start()
    out_ref[...] = os_[...].reshape(out_ref.shape).astype(BF16)
    dq_ref[...] = dqs[...].reshape(dq_ref.shape).astype(BF16)
    gains_ref[0:1, :] = jnp.sum(qsum[...], axis=0, keepdims=True)
    gains_ref[1:2, :] = jnp.sum(ksum[...], axis=0, keepdims=True)
    for tile in range(PROMPT, tile_count):

        @pl.when((tile < wb) | (tile >= wb + WINDOW))
        def _(tile=tile):
            zero_copy(tile).wait()

    store_prompt.wait()
    store_window.wait()


def attend(tiles, rewards, seg, qgain, kgain, q, up, kv):
    local = q.shape[0]
    seq_len = kv.shape[0]
    blocks = local // HALF
    tile_count = seq_len // TILE
    cosine, sine = rope_tables(2 * PROMPT * TILE)
    vmem = pl.BlockSpec(memory_space=pltpu.VMEM)
    smem = pl.BlockSpec(memory_space=pltpu.SMEM)
    hbm = pl.BlockSpec(memory_space=pl.ANY)
    rows = local * HEADS
    span_rows = SPAN * TILE * 2 * KV
    cols = GROUP * HALF
    return pl.pallas_call(
        functools.partial(attention_kernel, blocks, tile_count),
        out_shape=(
            jax.ShapeDtypeStruct(q.shape, BF16),
            jax.ShapeDtypeStruct(q.shape, BF16),
            jax.ShapeDtypeStruct((2, WIDTH), F32),
            jax.ShapeDtypeStruct(kv.shape, BF16),
        ),
        in_specs=[smem, smem, vmem, vmem, vmem, vmem, vmem, vmem, vmem, hbm],
        out_specs=(vmem, vmem, vmem, hbm),
        scratch_shapes=[
            pltpu.SMEM((tile_count * tile_count,), jnp.int32),
            pltpu.VMEM((SPAN * TILE, 2 * KV, WIDTH), BF16),
            pltpu.VMEM((span_rows, WIDTH), F32),
            pltpu.VMEM((span_rows, WIDTH), F32),
            pltpu.VMEM((rows, WIDTH), F32),
            pltpu.VMEM((rows, WIDTH), F32),
            pltpu.VMEM((rows, WIDTH), F32),
            pltpu.VMEM((rows, WIDTH), F32),
            pltpu.VMEM((SPAN, TILE, WIDTH), BF16),
            pltpu.VMEM((SPAN, TILE, WIDTH), BF16),
            pltpu.VMEM((SPAN, TILE, WIDTH), BF16),
            pltpu.VMEM((SPAN, TILE, WIDTH), BF16),
            pltpu.VMEM((SPAN, TILE, WIDTH), F32),
            pltpu.VMEM((SPAN, TILE, WIDTH), F32),
            pltpu.VMEM((4, 2 * TILE, cols), F32),
            pltpu.VMEM((4, 2 * TILE, cols), BF16),
            pltpu.VMEM((8, WIDTH), F32),
            pltpu.VMEM((8, WIDTH), F32),
            pltpu.VMEM((TILE, 2 * KV, WIDTH), BF16),
            pltpu.SemaphoreType.DMA((2,)),
            pltpu.SemaphoreType.DMA((2 + tile_count,)),
        ],
        compiler_params=pltpu.CompilerParams(vmem_limit_bytes=48 * 1024 * 1024),
        name="tree_attention",
    )(tiles, rewards, seg, qgain, kgain, jnp.asarray(cosine), jnp.asarray(sine), q, up, kv)


def butterfly_sum(x, axis):
    size = lax.axis_size(axis)
    step = 1
    while step < size:
        x = x + lax.ppermute(x, axis, [(i, i ^ step) for i in range(size)])
        step *= 2
    return x


def per_device(q_proj, k_proj, v_proj, upstream, segment_ids, tree_tiles, rewards, q_gain, k_gain):
    kv = jnp.concatenate([k_proj[0], v_proj[0]], axis=1)
    kv_all = lax.all_gather(kv, "seq", tiled=True)
    out, dq, gains, dkv = attend(
        tree_tiles.reshape(-1),
        rewards[0],
        segment_ids,
        q_gain[None],
        k_gain[None],
        q_proj[0],
        upstream[0],
        kv_all,
    )
    gains = butterfly_sum(butterfly_sum(gains, "dp"), "seq")
    dkv = lax.psum_scatter(dkv, "seq", tiled=True)
    return (out[None], dq[None], dkv[None, :, :KV], dkv[None, :, KV:], gains[0], gains[1])


def solution(mesh):
    whole = P("dp", "seq", None, None)
    return jax.shard_map(
        per_device,
        mesh=mesh,
        in_specs=(whole, whole, whole, whole, P("dp", "seq"), P("dp", None, None), P("dp", None), P(), P()),
        out_specs=(whole, whole, whole, whole, P(), P()),
        check_vma=False,
    )
```

```python
import functools
import math

import jax
import jax.numpy as jnp
import numpy as np
from jax import lax
from jax.experimental import pallas as pl
from jax.experimental.pallas import tpu as pltpu
from jax.sharding import PartitionSpec as P

TILE = 128
PROMPT = 4
WINDOW = 5
SPAN = PROMPT + WINDOW
RESPONSES = 5
HEADS = 16
KV = 4
GROUP = HEADS // KV
WIDTH = 128
HALF = 64
BLOCKS = 3
COLS = GROUP * HALF
ALL = BLOCKS * COLS
LOCAL = BLOCKS * HALF
PAIR = 2 * KV
EPS = 1e-06
ROPE_BASE = 1000000.0
F32 = jnp.float32
BF16 = jnp.bfloat16
VMEM = pl.BlockSpec(memory_space=pltpu.VMEM)
SMEM = pl.BlockSpec(memory_space=pltpu.SMEM)
HBM = pl.BlockSpec(memory_space=pltpu.HBM)


def rope_tables(count):
    freq = np.exp(
        np.arange(WIDTH // 2, dtype=np.float32) * np.float32(-2.0 * math.log(ROPE_BASE) / WIDTH)
    ).astype(np.float32)
    angle = (np.arange(count, dtype=np.float32)[:, None] * freq[None, :]).astype(np.float64)
    cosine, sine = np.cos(angle), np.sin(angle)
    return (
        np.concatenate([cosine, cosine], axis=1).astype(np.float32),
        np.concatenate([-sine, sine], axis=1).astype(np.float32),
    )


def swap_halves(x):
    return pltpu.roll(x, WIDTH // 2, 1)


def mean_lanes(x):
    return jnp.sum(x, axis=1, keepdims=True) * (1.0 / WIDTH)


def rows_to_eight(x):
    return jnp.sum(x.reshape(-1, 8, WIDTH), axis=0)


def head_rows(i, g, h):
    return pl.ds(i * HALF * HEADS + GROUP * g + h, HALF, stride=HEADS)


def swap_rows(x):
    return jnp.concatenate([x[WIDTH // 2 :], x[: WIDTH // 2]], axis=0)


def mean_rows(x):
    return jnp.sum(x, axis=0, keepdims=True) * (1.0 / WIDTH)


def pack_kernel(k_hbm, v_hbm, kv_hbm, *rest):
    targets, (k_ref, v_ref, flat, kv_ref, in_sem, out_sem) = rest[:-6], rest[-6:]
    loads = [
        pltpu.make_async_copy(k_hbm, k_ref, in_sem.at[0]),
        pltpu.make_async_copy(v_hbm, v_ref, in_sem.at[1]),
    ]
    for load in loads:
        load.start()
    for n, ref in enumerate((k_ref, v_ref)):
        loads[n].wait()
        flat[...] = ref[...].astype(F32).reshape(flat.shape)
        for g in range(KV):
            kv_ref[n * KV + g] = flat[pl.ds(g, LOCAL, stride=KV), :].astype(BF16)
    stores = [pltpu.make_async_copy(kv_ref, kv_hbm, out_sem.at[0])]
    for b, target in enumerate(targets):
        size = target.shape[1]
        stores.append(
            pltpu.make_async_copy(kv_ref.at[:, pl.ds(b * size, size), :], target, out_sem.at[1 + b])
        )
    for store in stores:
        store.start()
    for store in stores:
        store.wait()


def prepare_kernel(
    place_ref, rewards_ref, seg_ref, gain_ref, cos_ref, sin_ref, q_ref, up_ref, k_ref,
    query_hbm, query_t_hbm, grad_hbm, grad_t_hbm, unit_hbm, factor_hbm, angle_hbm, own_hbm, xq, xu,
    query_ref, query_t_ref, grad_ref, grad_t_ref, unit_ref, factor_ref, angle_ref, own_ref, out_sem,
):
    xq[...] = q_ref[...].astype(F32).reshape(xq.shape)
    xu[...] = up_ref[...].astype(F32).reshape(xu.shape)
    gain = gain_ref[...]
    reward = [rewards_ref[r] for r in range(RESPONSES)]
    centre = (reward[0] + reward[1] + reward[2] + reward[3] + reward[4]) * (1.0 / RESPONSES)
    seg = seg_ref[...]
    adv_row = jnp.zeros(seg.shape, F32)
    for r in range(RESPONSES):
        adv_row = adv_row + jnp.where(seg == r + 1, reward[r] - centre, 0.0)
    for i in range(BLOCKS):
        block = BLOCKS * lax.axis_index("seq") + i
        start = place_ref[block // 2] * TILE + lax.rem(block, 2) * HALF
        start = pl.multiple_of(start, HALF)
        for n, ref in enumerate((cos_ref, sin_ref)):
            angle = ref[pl.ds(start, HALF), :]
            angle_ref[n, :, i * COLS : (i + 1) * COLS] = jnp.concatenate([angle] * GROUP, axis=0).T
            own_ref[n, i * HALF : (i + 1) * HALF, :] = angle
    for g in range(KV):
        x = k_ref[g].astype(F32)
        factor = lax.rsqrt(mean_lanes(x * x) + EPS)
        own_ref[2 + g] = x * factor
        own_ref[2 + KV + g] = jnp.broadcast_to(factor, (LOCAL, WIDTH))

    def per_kv(g, carry):
        for i in range(BLOCKS):
            span = slice(i * COLS, (i + 1) * COLS)

            def columns(ref):
                rows = [ref[head_rows(i, g, h), :] for h in range(GROUP)]
                return jnp.concatenate(rows, axis=0).T

            x = columns(xq)
            factor = lax.rsqrt(mean_rows(x * x) + EPS)
            unit = x * factor
            normed = unit * gain
            turned = normed * angle_ref[0, :, span] + swap_rows(normed) * angle_ref[1, :, span]
            query_ref[g, span, :] = turned.T.astype(BF16)
            query_t_ref[g, :, span] = turned.astype(BF16)
            unit_ref[g, :, span] = unit
            factor_ref[g, :, span] = jnp.broadcast_to(factor, (8, COLS))
            adv = jnp.concatenate([adv_row[:, i * HALF : (i + 1) * HALF]] * GROUP, axis=1)
            grad = columns(xu) * adv
            grad_t_ref[g, :, span] = grad.astype(BF16)
            grad_ref[g, span, :] = grad.T.astype(BF16)
        return carry

    lax.fori_loop(0, KV, per_kv, 0)
    stores = [
        pltpu.make_async_copy(source, target, out_sem.at[n])
        for n, (source, target) in enumerate(
            [
                (query_ref, query_hbm), (query_t_ref, query_t_hbm), (grad_ref, grad_hbm),
                (grad_t_ref, grad_t_hbm), (unit_ref, unit_hbm), (factor_ref, factor_hbm),
                (angle_ref, angle_hbm), (own_ref, own_hbm),
            ]
        )
    ]
    for store in stores:
        store.start()
    for store in stores:
        store.wait()


def attention_kernel(
    tile_count, table_ref, place_ref, gain_ref, cos_hbm, sin_hbm,
    query_hbm, query_t_hbm, grad_hbm, grad_t_hbm, unit_hbm, angle_hbm,
    parts_hbm, mine_hbm, hop_in_hbm, swap_in_hbm,
    out_hbm, dq_hbm, gain_out_ref, prompt_hbm, swap_hbm, hop_hbm, own_hbm,
    out_ref, dq_ref, cos_ref, sin_ref, query_v, query_t_v, grad_v, grad_t_v, unit_v, angle_v,
    kvb, ybuf, kr, kt, vr, vt, kcos, ksin, ebuf, pbuf, dsbuf, limits, ksum, lsum, qsum,
    in_sem, out_sem,
):
    me = lax.axis_index("seq")
    wb = jnp.clip((BLOCKS * me) // 2 - 3, PROMPT, tile_count - WINDOW)
    prompt_rows = PROMPT * TILE

    def rows_of(back, skip=0):
        return pl.multiple_of((me - back) * LOCAL + skip - wb * TILE + 2 * prompt_rows, HALF)

    kvb[:, 2 * prompt_rows :, :] = jnp.zeros((PAIR, WINDOW * TILE, WIDTH), BF16)
    devices, _, share_rows, _ = parts_hbm.shape
    key_loads = [
        pltpu.make_async_copy(
            parts_hbm.at[n], kvb.at[:, pl.ds(n * share_rows, share_rows), :], in_sem.at[8 + n]
        )
        for n in range(devices)
    ]
    key_loads.append(pltpu.make_async_copy(cos_hbm, cos_ref, in_sem.at[6]))
    key_loads.append(pltpu.make_async_copy(sin_hbm, sin_ref, in_sem.at[7]))
    window_loads = [
        (0, pltpu.make_async_copy(mine_hbm, kvb.at[:, pl.ds(rows_of(0), LOCAL), :], in_sem.at[8 + devices]))
    ]

    def earlier(back, source, skip, size):
        start = jnp.maximum(rows_of(back, skip), prompt_rows)
        target = kvb.at[:, pl.ds(pl.multiple_of(start, HALF), size), :]
        window_loads.append((back, pltpu.make_async_copy(source, target, in_sem.at[8 + devices + back])))

    earlier(1, swap_in_hbm.at[:, pl.ds(0, LOCAL), :], 0, LOCAL)
    earlier(2, hop_in_hbm, 0, LOCAL)
    earlier(3, swap_in_hbm.at[:, pl.ds(LOCAL, HALF), :], LOCAL - HALF, HALF)
    loads = [
        pltpu.make_async_copy(query_t_hbm, query_t_v, in_sem.at[0]),
        pltpu.make_async_copy(grad_t_hbm, grad_t_v, in_sem.at[1]),
        pltpu.make_async_copy(query_hbm, query_v, in_sem.at[2]),
        pltpu.make_async_copy(grad_hbm, grad_v, in_sem.at[3]),
        pltpu.make_async_copy(unit_hbm, unit_v, in_sem.at[4]),
        pltpu.make_async_copy(angle_hbm, angle_v, in_sem.at[5]),
    ]
    for load in key_loads + loads:
        load.start()
    for back, load in window_loads:
        pl.when(me >= back)(load.start)

    gain = gain_ref[...]
    gain_turned = swap_halves(gain)
    ksum[...] = jnp.zeros_like(ksum)
    lsum[...] = jnp.zeros_like(lsum)
    qsum[...] = jnp.zeros_like(qsum)
    ybuf[:, prompt_rows : 2 * prompt_rows] = jnp.zeros((PAIR, prompt_rows, WIDTH), BF16)

    lane = lax.broadcasted_iota(jnp.int32, (1, COLS), 1)
    key_place = [tile * TILE for tile in range(PROMPT)]
    key_place += [pl.multiple_of(place_ref[wb + j] * TILE, TILE) for j in range(WINDOW)]
    for tile in range(SPAN):
        name = tile if tile < PROMPT else wb + tile - PROMPT
        for i in range(BLOCKS):
            block = BLOCKS * me + i
            kind = table_ref[(block // 2) * tile_count + name]
            one = (kind == 1).astype(jnp.int32)
            two = (kind == 2).astype(jnp.int32)
            slot = lax.rem(block, 2) * HALF + lax.rem(lane, HALF)
            limits[tile : tile + 1, i * COLS : (i + 1) * COLS] = (
                two * slot + (one * (TILE + 1) - 1 + two)
            )

    for load in key_loads:
        load.wait()
    for back, load in window_loads:
        pl.when(me >= back)(load.wait)

    def prepare_keys(g, carry):
        for tile in range(SPAN):
            at = slice(tile * TILE, (tile + 1) * TILE)
            source = tile * TILE if tile < PROMPT else tile * TILE + prompt_rows
            source = slice(source, source + TILE)
            x = kvb[g, source, :].astype(F32)
            factor = lax.rsqrt(mean_lanes(x * x) + EPS)
            unit = x * factor
            first = unit * cos_ref[pl.ds(key_place[tile], TILE), :]
            second = swap_halves(unit) * sin_ref[pl.ds(key_place[tile], TILE), :]
            turned = first * gain + second * gain_turned
            kcos[g, at, :] = first
            ksin[g, at, :] = second
            kr[g, at, :] = turned.astype(BF16)
            kt[g, :, at] = turned.T.astype(BF16)
            value = kvb[KV + g, source, :]
            vr[g, at, :] = value
            vt[g, :, at] = value.astype(F32).T.astype(BF16)
        return carry

    lax.fori_loop(0, KV, prepare_keys, 0)
    for load in loads:
        load.wait()

    scale = 1.0 / math.sqrt(WIDTH)
    key_at = lax.broadcasted_iota(jnp.int32, (TILE, ALL), 0)
    third = SPAN // 3

    def per_kv(g, carry):
        query_t = query_t_v[g]
        grad_t = grad_t_v[g]
        total = jnp.zeros((1, ALL), F32)
        for c in range(3):
            rows = slice(c * third * TILE, (c + 1) * third * TILE)
            score = jnp.dot(kr[g, rows, :], query_t, preferred_element_type=F32)
            for t in range(third):
                tile = c * third + t
                raw = jnp.where(
                    key_at <= limits[tile : tile + 1, :],
                    jnp.exp2(score[t * TILE : (t + 1) * TILE] * (scale * math.log2(math.e))),
                    0.0,
                )
                ebuf[tile * TILE : (tile + 1) * TILE, :] = raw
                total = total + jnp.sum(raw, axis=0, keepdims=True)
        share = jnp.where(total > 0, 1.0 / total, 0.0)
        for tile in range(SPAN):
            at = slice(tile * TILE, (tile + 1) * TILE)
            pbuf[at, :] = (ebuf[at, :] * share).astype(BF16)
        out_t = jnp.dot(vt[g], pbuf[...], preferred_element_type=F32)
        out_ref[g] = out_t.astype(BF16)
        delta = jnp.sum(grad_t.astype(F32) * out_t, axis=0, keepdims=True)
        for c in range(3):
            rows = slice(c * third * TILE, (c + 1) * third * TILE)
            dweights = jnp.dot(vr[g, rows, :], grad_t, preferred_element_type=F32)
            dsbuf[rows, :] = (
                pbuf[rows, :].astype(F32) * (dweights - delta)
            ).astype(BF16)
        dv = jnp.dot(pbuf[...], grad_v[g], preferred_element_type=F32)
        dq_t = jnp.dot(kt[g], dsbuf[...], preferred_element_type=F32)
        dq_t = (dq_t * scale).astype(BF16)
        dq_ref[g] = dq_t
        dq_t = dq_t.astype(F32)
        dnormed = (dq_t * angle_v[0] - swap_rows(dq_t) * angle_v[1]) * unit_v[g]
        for n in range(ALL // WIDTH):
            qsum[...] += dnormed[:, n * WIDTH : (n + 1) * WIDTH]
        dk = jnp.dot(dsbuf[...], query_v[g], preferred_element_type=F32) * scale
        ksum[...] += rows_to_eight(dk * kcos[g])
        lsum[...] += rows_to_eight(dk * ksin[g])
        for at, item in ((g, dk), (KV + g, dv)):
            item = item.astype(BF16)
            ybuf[at, :prompt_rows, :] = item[:prompt_rows]
            ybuf[at, 2 * prompt_rows :, :] = item[prompt_rows:]
        pltpu.make_async_copy(out_ref.at[g], out_hbm.at[g], out_sem.at[g]).start()
        pltpu.make_async_copy(dq_ref.at[g], dq_hbm.at[g], out_sem.at[KV + g]).start()
        return carry

    lax.fori_loop(0, KV, per_kv, 0)

    def mine(back, skip=0):
        return pl.multiple_of(jnp.maximum(rows_of(back, skip), prompt_rows), HALF)

    stores = [(n * share_rows, share_rows, prompt_hbm.at[n]) for n in range(devices)]
    stores += [
        (mine(1), LOCAL, swap_hbm.at[:, pl.ds(0, LOCAL), :]),
        (mine(3, LOCAL - HALF), HALF, swap_hbm.at[:, pl.ds(LOCAL, HALF), :]),
        (mine(2), LOCAL, hop_hbm),
        (mine(0), LOCAL, own_hbm),
    ]
    stores = [
        pltpu.make_async_copy(ybuf.at[:, pl.ds(start, size), :], target, out_sem.at[PAIR + n])
        for n, (start, size, target) in enumerate(stores)
    ]
    for store in stores:
        store.start()
    gain_out_ref[0:1, :] = jnp.sum(qsum[...].T, axis=0, keepdims=True)
    second = swap_halves(jnp.sum(lsum[...], axis=0, keepdims=True))
    gain_out_ref[1:2, :] = jnp.sum(ksum[...], axis=0, keepdims=True) + second
    for g in range(KV):
        pltpu.make_async_copy(out_ref.at[g], out_hbm.at[g], out_sem.at[g]).wait()
        pltpu.make_async_copy(dq_ref.at[g], dq_hbm.at[g], out_sem.at[KV + g]).wait()
    for store in stores:
        store.wait()


def finish_kernel(
    gain_ref, angle_ref, out_t_ref, dq_t_ref, unit_ref, factor_ref, out_ref, dq_ref, os_, dqs,
):
    gain = gain_ref[...]

    def per_kv(g, carry):
        for i in range(BLOCKS):
            span = slice(i * COLS, (i + 1) * COLS)
            out = out_t_ref[g, :, span].astype(F32).T
            dturned = dq_t_ref[g, :, span].astype(F32)
            dnormed = dturned * angle_ref[0, :, span] - swap_rows(dturned) * angle_ref[1, :, span]
            unit = unit_ref[g, :, span]
            dunit = dnormed * gain
            dx = (factor_ref[g, 0:1, span] * (dunit - unit * mean_rows(dunit * unit))).T
            for h in range(GROUP):
                os_[head_rows(i, g, h), :] = out[h * HALF : (h + 1) * HALF]
                dqs[head_rows(i, g, h), :] = dx[h * HALF : (h + 1) * HALF]
        return carry

    lax.fori_loop(0, KV, per_kv, 0)
    out_ref[...] = os_[...].reshape(out_ref.shape).astype(BF16)
    dq_ref[...] = dqs[...].reshape(dq_ref.shape).astype(BF16)


def last_kernel(
    gain_ref, key_ref, own_ref, swap_ref, back_ref, *rest,
):
    blocks, (dk_ref, dv_ref, flat) = rest[:-3], rest[-3:]
    gain = gain_ref[...]
    even = (1 - lax.rem(lax.axis_index("seq"), 2)).astype(F32)

    for ref, first in ((dk_ref, 0), (dv_ref, KV)):
        for g in range(KV):
            at = first + g
            prompt = jnp.concatenate([block[at] for block in blocks], axis=0).astype(F32)
            summed = own_ref[at].astype(F32) + back_ref[at].astype(F32) + prompt
            summed = summed + even * swap_ref[at, :LOCAL].astype(F32)
            if first == 0:
                dnormed = summed * key_ref[0] - swap_halves(summed) * key_ref[1]
                unit = key_ref[2 + g]
                dunit = dnormed * gain
                summed = key_ref[2 + KV + g] * (dunit - unit * mean_lanes(dunit * unit))
            flat[pl.ds(g, LOCAL, stride=KV), :] = summed
        ref[...] = flat[...].reshape(ref.shape).astype(BF16)


def shape(dims, dtype=BF16):
    return jax.ShapeDtypeStruct(dims, dtype)


def cost(flops, size):
    return pl.CostEstimate(flops=flops, bytes_accessed=size, transcendentals=0)


def params(mib):
    return pltpu.CompilerParams(vmem_limit_bytes=mib * 1024 * 1024)


def pack(k, v, share):
    blocks = LOCAL // share
    return pl.pallas_call(
        pack_kernel,
        out_shape=[shape((PAIR, LOCAL, WIDTH))] + [shape((PAIR, share, WIDTH))] * blocks,
        in_specs=[HBM] * 2,
        out_specs=[HBM] * (1 + blocks),
        scratch_shapes=[
            pltpu.VMEM(k.shape, BF16), pltpu.VMEM(k.shape, BF16), pltpu.VMEM((LOCAL * KV, WIDTH), F32),
            pltpu.VMEM((PAIR, LOCAL, WIDTH), BF16),
            pltpu.SemaphoreType.DMA((2,)), pltpu.SemaphoreType.DMA((1 + blocks,)),
        ],
        compiler_params=params(32),
        cost_estimate=cost(1_000_000, 2_000_000),
        name="pack_keys",
    )(k, v)


def prepare(place, rewards, seg, gain, cosine, sine, q, up, k):
    rows = (KV, ALL, WIDTH)
    cols = (KV, WIDTH, ALL)
    shapes = [
        (rows, BF16), (cols, BF16), (rows, BF16), (cols, BF16), (cols, F32), ((KV, 8, ALL), F32),
        ((2, WIDTH, ALL), F32), ((2 + PAIR, LOCAL, WIDTH), F32),
    ]
    return pl.pallas_call(
        prepare_kernel,
        out_shape=[shape(*item) for item in shapes],
        in_specs=[SMEM, SMEM] + [VMEM] * 7,
        out_specs=[HBM] * 8,
        scratch_shapes=[pltpu.VMEM((LOCAL * HEADS, WIDTH), F32)] * 2
        + [pltpu.VMEM(*item) for item in shapes]
        + [pltpu.SemaphoreType.DMA((8,))],
        compiler_params=params(32),
        cost_estimate=cost(100_000_000, 16_000_000),
        name="prepare_queries",
    )(place, rewards, seg, gain, cosine, sine, q, up, k)


def attend(table, place, gain, cosine, sine, *operands):
    angle, parts = operands[5:7]
    devices, _, share, _ = parts.shape
    tile_count = devices * LOCAL // TILE
    span_rows = SPAN * TILE
    rows = (KV, ALL, WIDTH)
    cols = (KV, WIDTH, ALL)
    keys = (KV, span_rows, WIDTH)
    keys_t = (KV, WIDTH, span_rows)
    return pl.pallas_call(
        functools.partial(attention_kernel, tile_count),
        out_shape=(
            shape(cols), shape(cols), shape((2, WIDTH), F32),
            shape((devices, PAIR, share, WIDTH)),
            shape((PAIR, LOCAL + HALF, WIDTH)), shape((PAIR, LOCAL, WIDTH)), shape((PAIR, LOCAL, WIDTH)),
        ),
        in_specs=[SMEM, SMEM, VMEM] + [HBM] * 12,
        out_specs=(HBM, HBM, VMEM) + (HBM,) * 4,
        scratch_shapes=[
            pltpu.VMEM(cols, BF16), pltpu.VMEM(cols, BF16),
            pltpu.VMEM(cosine.shape, F32), pltpu.VMEM(cosine.shape, F32),
            pltpu.VMEM(rows, BF16), pltpu.VMEM(cols, BF16), pltpu.VMEM(rows, BF16), pltpu.VMEM(cols, BF16),
            pltpu.VMEM(cols, F32), pltpu.VMEM(angle.shape, F32),
            pltpu.VMEM((PAIR, span_rows + PROMPT * TILE, WIDTH), BF16),
            pltpu.VMEM((PAIR, span_rows + PROMPT * TILE, WIDTH), BF16),
            pltpu.VMEM(keys, BF16), pltpu.VMEM(keys_t, BF16), pltpu.VMEM(keys, BF16), pltpu.VMEM(keys_t, BF16),
            pltpu.VMEM(keys, F32), pltpu.VMEM(keys, F32),
            pltpu.VMEM((span_rows, ALL), F32),
            pltpu.VMEM((span_rows, ALL), BF16), pltpu.VMEM((span_rows, ALL), BF16),
            pltpu.VMEM((16, ALL), jnp.int32),
            pltpu.VMEM((8, WIDTH), F32), pltpu.VMEM((8, WIDTH), F32), pltpu.VMEM((WIDTH, WIDTH), F32),
            pltpu.SemaphoreType.DMA((12 + devices,)), pltpu.SemaphoreType.DMA((devices + 4 + PAIR,)),
        ],
        compiler_params=params(56),
        cost_estimate=cost(12 * span_rows * ALL * WIDTH * KV, 12_000_000),
        name="tree_attention",
    )(table, place, gain, cosine, sine, *operands)


def finish(gain, angle, out_t, dq_t, unit, factor):
    dims = (LOCAL, HEADS, WIDTH)
    return pl.pallas_call(
        finish_kernel,
        out_shape=(shape(dims), shape(dims)),
        in_specs=[VMEM] * 6,
        out_specs=(VMEM,) * 2,
        scratch_shapes=[pltpu.VMEM((LOCAL * HEADS, WIDTH), F32)] * 2,
        compiler_params=params(32),
        cost_estimate=cost(100_000_000, 10_000_000),
        name="finish_queries",
    )(gain, angle, out_t, dq_t, unit, factor)


def last(gain, key, own, swap, back, blocks):
    dims = (LOCAL, KV, WIDTH)
    return pl.pallas_call(
        last_kernel,
        out_shape=(shape(dims), shape(dims)),
        in_specs=[VMEM] * (5 + len(blocks)),
        out_specs=(VMEM,) * 2,
        scratch_shapes=[pltpu.VMEM((LOCAL * KV, WIDTH), F32)],
        compiler_params=params(32),
        cost_estimate=cost(1_000_000, 4_000_000),
        name="finish_keys",
    )(gain, key, own, swap, back, *blocks)


def tile_table(tiles, count):
    ids = jnp.arange(count, dtype=jnp.int32)
    row_hits = (tiles[:, 0, None] == ids).astype(jnp.int32) * tiles[:, 2, None]
    col_hits = (tiles[:, 1, None] == ids).astype(jnp.int32)
    table = jnp.einsum("tq,tk->qk", row_hits, col_hits)
    live = (table > 0) & (ids[None, :] >= PROMPT)
    first = jnp.min(jnp.where(live, ids[None, :], count), axis=1)
    inside = (ids >= PROMPT) & (first < count)
    place = jnp.minimum(jnp.where(inside, PROMPT + ids - first, ids), 2 * PROMPT - 1)
    return table.reshape(-1), place


def sum_four(x, axis, step):
    size = lax.axis_size(axis)
    if size <= step:
        return x
    a, b, c = (
        lax.ppermute(x, axis, [(i, i ^ (n * step)) for i in range(size)]) for n in (1, 2, 3)
    )
    return (x + a) + (b + c)


def prompt_pairs(devices, per_owner):
    routes = []
    for b in range(per_owner):
        pairs = [(owner, owner * per_owner + b) for owner in range(3)]
        routes.append([pair for pair in pairs if pair[1] < devices])
    return routes


def per_device(q_proj, k_proj, v_proj, upstream, segment_ids, tree_tiles, rewards, q_gain, k_gain):
    devices = lax.axis_size("seq")
    share = PROMPT * TILE // devices
    tile_count = devices * LOCAL // TILE
    routes = prompt_pairs(devices, LOCAL // share)
    even = lax.rem(lax.axis_index("seq"), 2) == 0
    cores = [(i, i ^ 1) for i in range(devices)]

    kv, *blocks = pack(k_proj[0], v_proj[0], share)
    mine = [lax.ppermute(block, "seq", pairs) for block, pairs in zip(blocks, routes)]
    hop_in = lax.ppermute(kv, "seq", [(i, i + 2) for i in range(devices - 2)])
    mine = mine[0] + mine[1] + mine[2] + mine[3] + mine[4] + mine[5]
    mine, hop_in = lax.optimization_barrier((mine, hop_in))
    parts = lax.all_to_all(
        jnp.broadcast_to(mine[None], (devices,) + mine.shape), "seq", split_axis=0, concat_axis=0, tiled=True
    )
    swap_in = jnp.where(
        even,
        jnp.concatenate([kv, hop_in[:, LOCAL - HALF :]], axis=1),
        jnp.concatenate([hop_in, hop_in[:, LOCAL - HALF :]], axis=1),
    )
    swap_in = lax.ppermute(swap_in, "seq", cores)

    table, place = tile_table(tree_tiles[0], tile_count)
    cosine, sine = (jnp.asarray(item) for item in rope_tables(2 * PROMPT * TILE))
    query, query_t, grad, grad_t, unit, factor, angle, own_key = prepare(
        place, rewards[0], segment_ids, q_gain[:, None], cosine, sine, q_proj[0], upstream[0],
        kv[:KV],
    )
    out_t, dq_t, gains, prompt, swap, hop, own = attend(
        table, place, k_gain[None], cosine, sine, query, query_t, grad, grad_t, unit, angle,
        parts, kv, hop_in, swap_in,
    )

    parts = lax.all_to_all(prompt, "seq", split_axis=0, concat_axis=0, tiled=True)
    swap = lax.ppermute(swap, "seq", cores)
    far = jnp.concatenate([jnp.zeros((PAIR, LOCAL - HALF, WIDTH), BF16), swap[:, LOCAL:]], axis=1)
    hop = hop + jnp.where(even, far, swap[:, :LOCAL])
    back = lax.ppermute(hop, "seq", [(i, i - 2) for i in range(2, devices)])
    gains = sum_four(gains, "dp", 1)
    gains, out_t, dq_t = lax.optimization_barrier((gains, out_t, dq_t))
    out, dq = finish(q_gain[:, None], angle, out_t, dq_t, unit, factor)
    gains = sum_four(sum_four(gains, "dp", 4), "seq", 1)
    piece = jnp.sum(parts.astype(F32), axis=0).astype(BF16)
    piece, gains, out, dq = lax.optimization_barrier((piece, gains, out, dq))
    blocks = [lax.ppermute(piece, "seq", [(b, a) for a, b in pairs]) for pairs in routes]
    gains = sum_four(gains, "seq", 4)
    dk, dv = last(k_gain[None], own_key, own, swap, back, blocks)
    return (out[None], dq[None], dk[None], dv[None], gains[0], gains[1])


def solution(mesh):
    whole = P("dp", "seq", None, None)
    return jax.shard_map(
        per_device,
        mesh=mesh,
        in_specs=(whole, whole, whole, whole, P("dp", "seq"), P("dp", None, None), P("dp", None), P(), P()),
        out_specs=(whole, whole, whole, whole, P(), P()),
        check_vma=False,
    )
```

```python
import functools
import math

import jax
import jax.numpy as jnp
import numpy as np
from jax import lax
from jax.experimental import pallas as pl
from jax.experimental.pallas import tpu as pltpu
from jax.sharding import PartitionSpec as P

TILE = 128
PROMPT = 4
WINDOW = 5
SPAN = PROMPT + WINDOW
RESPONSES = 5
HEADS = 16
KV = 4
GROUP = HEADS // KV
WIDTH = 128
HALF = 64
BLOCKS = 3
COLS = GROUP * HALF
ALL = BLOCKS * COLS
LOCAL = BLOCKS * HALF
PAIR = 2 * KV
EPS = 1e-06
ROPE_BASE = 1000000.0
F32 = jnp.float32
BF16 = jnp.bfloat16
VMEM = pl.BlockSpec(memory_space=pltpu.VMEM)
SMEM = pl.BlockSpec(memory_space=pltpu.SMEM)
HBM = pl.BlockSpec(memory_space=pltpu.HBM)


def rope_tables(count):
    freq = np.exp(
        np.arange(WIDTH // 2, dtype=np.float32) * np.float32(-2.0 * math.log(ROPE_BASE) / WIDTH)
    ).astype(np.float32)
    angle = (np.arange(count, dtype=np.float32)[:, None] * freq[None, :]).astype(np.float64)
    cosine, sine = np.cos(angle), np.sin(angle)
    return (
        np.concatenate([cosine, cosine], axis=1).astype(np.float32),
        np.concatenate([-sine, sine], axis=1).astype(np.float32),
    )


def swap_halves(x):
    return pltpu.roll(x, WIDTH // 2, 1)


def mean_lanes(x):
    return jnp.sum(x, axis=1, keepdims=True) * (1.0 / WIDTH)


def rows_to_eight(x):
    return jnp.sum(x.reshape(-1, 8, WIDTH), axis=0)


def head_rows(i, g, h):
    return pl.ds(i * HALF * HEADS + GROUP * g + h, HALF, stride=HEADS)


def swap_rows(x):
    return jnp.concatenate([x[WIDTH // 2 :], x[: WIDTH // 2]], axis=0)


def mean_rows(x):
    return jnp.sum(x, axis=0, keepdims=True) * (1.0 / WIDTH)


def pack_kernel(k_hbm, v_hbm, kv_hbm, *rest):
    targets, (k_ref, v_ref, flat, kv_ref, in_sem, out_sem) = rest[:-6], rest[-6:]
    loads = [
        pltpu.make_async_copy(k_hbm, k_ref, in_sem.at[0]),
        pltpu.make_async_copy(v_hbm, v_ref, in_sem.at[1]),
    ]
    for load in loads:
        load.start()
    for n, ref in enumerate((k_ref, v_ref)):
        loads[n].wait()
        flat[...] = ref[...].astype(F32).reshape(flat.shape)
        for g in range(KV):
            kv_ref[n * KV + g] = flat[pl.ds(g, LOCAL, stride=KV), :].astype(BF16)
    stores = [pltpu.make_async_copy(kv_ref, kv_hbm, out_sem.at[0])]
    for b, target in enumerate(targets):
        size = target.shape[1]
        stores.append(
            pltpu.make_async_copy(kv_ref.at[:, pl.ds(b * size, size), :], target, out_sem.at[1 + b])
        )
    for store in stores:
        store.start()
    for store in stores:
        store.wait()


def load_all(pairs, sems):
    loads = [pltpu.make_async_copy(a, b, sems.at[n]) for n, (a, b) in enumerate(pairs)]
    for load in loads:
        load.start()
    for load in loads:
        load.wait()


def prepare_kernel(
    place_ref, rewards_ref, seg_ref, gain_ref, cos_hbm, sin_hbm, q_hbm, up_hbm, k_hbm,
    query_hbm, query_t_hbm, grad_hbm, grad_t_hbm, unit_hbm, factor_hbm, angle_hbm, own_hbm, xq, xu,
    query_ref, query_t_ref, grad_ref, grad_t_ref, unit_ref, factor_ref, angle_ref, own_ref,
    cos_ref, sin_ref, q_ref, up_ref, k_ref, in_sem, out_sem,
):
    load_all(
        [(q_hbm, q_ref), (up_hbm, up_ref), (cos_hbm, cos_ref), (sin_hbm, sin_ref), (k_hbm.at[pl.ds(0, KV)], k_ref)],
        in_sem,
    )
    xq[...] = q_ref[...].astype(F32).reshape(xq.shape)
    xu[...] = up_ref[...].astype(F32).reshape(xu.shape)
    gain = gain_ref[...]
    reward = [rewards_ref[r] for r in range(RESPONSES)]
    centre = (reward[0] + reward[1] + reward[2] + reward[3] + reward[4]) * (1.0 / RESPONSES)
    seg = seg_ref[...]
    adv_row = jnp.zeros(seg.shape, F32)
    for r in range(RESPONSES):
        adv_row = adv_row + jnp.where(seg == r + 1, reward[r] - centre, 0.0)
    for i in range(BLOCKS):
        block = BLOCKS * lax.axis_index("seq") + i
        start = place_ref[block // 2] * TILE + lax.rem(block, 2) * HALF
        start = pl.multiple_of(start, HALF)
        for n, ref in enumerate((cos_ref, sin_ref)):
            angle = ref[pl.ds(start, HALF), :]
            angle_ref[n, :, i * COLS : (i + 1) * COLS] = jnp.concatenate([angle] * GROUP, axis=0).T
            own_ref[n, i * HALF : (i + 1) * HALF, :] = angle
    for g in range(KV):
        x = k_ref[g].astype(F32)
        factor = lax.rsqrt(mean_lanes(x * x) + EPS)
        own_ref[2 + g] = x * factor
        own_ref[2 + KV + g] = jnp.broadcast_to(factor, (LOCAL, WIDTH))

    def per_kv(g, carry):
        for i in range(BLOCKS):
            span = slice(i * COLS, (i + 1) * COLS)

            def columns(ref):
                rows = [ref[head_rows(i, g, h), :] for h in range(GROUP)]
                return jnp.concatenate(rows, axis=0).T

            x = columns(xq)
            factor = lax.rsqrt(mean_rows(x * x) + EPS)
            unit = x * factor
            normed = unit * gain
            turned = normed * angle_ref[0, :, span] + swap_rows(normed) * angle_ref[1, :, span]
            query_ref[g, span, :] = turned.T.astype(BF16)
            query_t_ref[g, :, span] = turned.astype(BF16)
            unit_ref[g, :, span] = unit
            factor_ref[g, :, span] = jnp.broadcast_to(factor, (8, COLS))
            adv = jnp.concatenate([adv_row[:, i * HALF : (i + 1) * HALF]] * GROUP, axis=1)
            grad = columns(xu) * adv
            grad_t_ref[g, :, span] = grad.astype(BF16)
            grad_ref[g, span, :] = grad.T.astype(BF16)
        return carry

    lax.fori_loop(0, KV, per_kv, 0)
    stores = [
        pltpu.make_async_copy(source, target, out_sem.at[n])
        for n, (source, target) in enumerate(
            [
                (query_ref, query_hbm), (query_t_ref, query_t_hbm), (grad_ref, grad_hbm),
                (grad_t_ref, grad_t_hbm), (unit_ref, unit_hbm), (factor_ref, factor_hbm),
                (angle_ref, angle_hbm), (own_ref, own_hbm),
            ]
        )
    ]
    for store in stores:
        store.start()
    for store in stores:
        store.wait()


def attention_kernel(
    tile_count, table_ref, place_ref, gain_ref, cos_hbm, sin_hbm,
    query_hbm, query_t_hbm, grad_hbm, grad_t_hbm, unit_hbm, angle_hbm,
    parts_hbm, others_hbm, mine_hbm, hop_in_hbm, swap_in_hbm,
    out_hbm, dq_hbm, gain_out_ref, keep_hbm, send_hbm, swap_hbm, hop_hbm, own_hbm,
    out_ref, dq_ref, cos_ref, sin_ref, query_v, query_t_v, grad_v, grad_t_v, unit_v, angle_v,
    kvb, ybuf, kr, kt, vr, vt, kcos, ksin, ebuf, pbuf, dsbuf, limits, ksum, lsum, qsum,
    in_sem, out_sem,
):
    me = lax.axis_index("seq")
    wb = jnp.clip((BLOCKS * me) // 2 - 3, PROMPT, tile_count - WINDOW)
    prompt_rows = PROMPT * TILE

    def rows_of(back, skip=0):
        return pl.multiple_of((me - back) * LOCAL + skip - wb * TILE + 2 * prompt_rows, HALF)

    kvb[:, 2 * prompt_rows :, :] = jnp.zeros((PAIR, WINDOW * TILE, WIDTH), BF16)
    chips, _, share_rows, _ = parts_hbm.shape
    devices = 2 * chips
    parity = lax.rem(me, 2)
    key_loads = []
    for n in range(chips):
        for at, half, source in ((2 * n, parity, parts_hbm), (2 * n + 1, 1 - parity, others_hbm)):
            start = pl.multiple_of(half * (prompt_rows // 2) + n * share_rows, share_rows)
            target = kvb.at[:, pl.ds(start, share_rows), :]
            key_loads.append(pltpu.make_async_copy(source.at[n], target, in_sem.at[8 + at]))
    key_loads.append(pltpu.make_async_copy(cos_hbm, cos_ref, in_sem.at[6]))
    key_loads.append(pltpu.make_async_copy(sin_hbm, sin_ref, in_sem.at[7]))
    window_loads = [
        (0, pltpu.make_async_copy(mine_hbm, kvb.at[:, pl.ds(rows_of(0), LOCAL), :], in_sem.at[8 + devices]))
    ]

    def earlier(back, source, skip, size):
        start = jnp.maximum(rows_of(back, skip), prompt_rows)
        target = kvb.at[:, pl.ds(pl.multiple_of(start, HALF), size), :]
        window_loads.append((back, pltpu.make_async_copy(source, target, in_sem.at[8 + devices + back])))

    earlier(1, swap_in_hbm.at[:, pl.ds(0, LOCAL), :], 0, LOCAL)
    earlier(2, hop_in_hbm, 0, LOCAL)
    earlier(3, swap_in_hbm.at[:, pl.ds(LOCAL, HALF), :], LOCAL - HALF, HALF)
    loads = [
        pltpu.make_async_copy(query_t_hbm, query_t_v, in_sem.at[0]),
        pltpu.make_async_copy(grad_t_hbm, grad_t_v, in_sem.at[1]),
        pltpu.make_async_copy(query_hbm, query_v, in_sem.at[2]),
        pltpu.make_async_copy(grad_hbm, grad_v, in_sem.at[3]),
        pltpu.make_async_copy(unit_hbm, unit_v, in_sem.at[4]),
        pltpu.make_async_copy(angle_hbm, angle_v, in_sem.at[5]),
    ]
    for load in key_loads:
        load.start()
    for back, load in window_loads:
        pl.when(me >= back)(load.start)

    gain = gain_ref[...]
    gain_turned = swap_halves(gain)
    ksum[...] = jnp.zeros_like(ksum)
    lsum[...] = jnp.zeros_like(lsum)
    qsum[...] = jnp.zeros_like(qsum)
    ybuf[:, prompt_rows : 2 * prompt_rows] = jnp.zeros((PAIR, prompt_rows, WIDTH), BF16)

    lane = lax.broadcasted_iota(jnp.int32, (1, COLS), 1)
    key_place = [tile * TILE for tile in range(PROMPT)]
    key_place += [pl.multiple_of(place_ref[wb + j] * TILE, TILE) for j in range(WINDOW)]
    for tile in range(SPAN):
        name = tile if tile < PROMPT else wb + tile - PROMPT
        for i in range(BLOCKS):
            block = BLOCKS * me + i
            kind = table_ref[(block // 2) * tile_count + name]
            one = (kind == 1).astype(jnp.int32)
            two = (kind == 2).astype(jnp.int32)
            slot = lax.rem(block, 2) * HALF + lax.rem(lane, HALF)
            limits[tile : tile + 1, i * COLS : (i + 1) * COLS] = (
                two * slot + (one * (TILE + 1) - 1 + two)
            )

    for load in key_loads:
        load.wait()
    for back, load in window_loads:
        pl.when(me >= back)(load.wait)
    for load in loads:
        load.start()

    def prepare_keys(g, carry):
        for tile in range(SPAN):
            at = slice(tile * TILE, (tile + 1) * TILE)
            source = tile * TILE if tile < PROMPT else tile * TILE + prompt_rows
            source = slice(source, source + TILE)
            x = kvb[g, source, :].astype(F32)
            factor = lax.rsqrt(mean_lanes(x * x) + EPS)
            unit = x * factor
            first = unit * cos_ref[pl.ds(key_place[tile], TILE), :]
            second = swap_halves(unit) * sin_ref[pl.ds(key_place[tile], TILE), :]
            turned = first * gain + second * gain_turned
            kcos[g, at, :] = first
            ksin[g, at, :] = second
            kr[g, at, :] = turned.astype(BF16)
            kt[g, :, at] = turned.T.astype(BF16)
            value = kvb[KV + g, source, :]
            vr[g, at, :] = value
            vt[g, :, at] = value.astype(F32).T.astype(BF16)
        return carry

    lax.fori_loop(0, KV, prepare_keys, 0)
    for load in loads:
        load.wait()

    scale = 1.0 / math.sqrt(WIDTH)
    key_at = lax.broadcasted_iota(jnp.int32, (TILE, ALL), 0)
    third = SPAN // 3

    def per_kv(g, carry):
        query_t = query_t_v[g]
        grad_t = grad_t_v[g]
        total = jnp.zeros((1, ALL), F32)
        for c in range(3):
            rows = slice(c * third * TILE, (c + 1) * third * TILE)
            score = jnp.dot(kr[g, rows, :], query_t, preferred_element_type=F32)
            for t in range(third):
                tile = c * third + t
                raw = jnp.where(
                    key_at <= limits[tile : tile + 1, :],
                    jnp.exp2(score[t * TILE : (t + 1) * TILE] * (scale * math.log2(math.e))),
                    0.0,
                )
                ebuf[tile * TILE : (tile + 1) * TILE, :] = raw
                total = total + jnp.sum(raw, axis=0, keepdims=True)
        share = jnp.where(total > 0, 1.0 / total, 0.0)
        for tile in range(SPAN):
            at = slice(tile * TILE, (tile + 1) * TILE)
            pbuf[at, :] = (ebuf[at, :] * share).astype(BF16)
        out_t = jnp.dot(vt[g], pbuf[...], preferred_element_type=F32)
        out_ref[g] = out_t.astype(BF16)
        delta = jnp.sum(grad_t.astype(F32) * out_t, axis=0, keepdims=True)
        for c in range(3):
            rows = slice(c * third * TILE, (c + 1) * third * TILE)
            dweights = jnp.dot(vr[g, rows, :], grad_t, preferred_element_type=F32)
            dsbuf[rows, :] = (
                pbuf[rows, :].astype(F32) * (dweights - delta)
            ).astype(BF16)
        dv = jnp.dot(pbuf[...], grad_v[g], preferred_element_type=F32)
        dq_t = jnp.dot(kt[g], dsbuf[...], preferred_element_type=F32)
        dq_t = (dq_t * scale).astype(BF16)
        dq_ref[g] = dq_t
        dq_t = dq_t.astype(F32)
        dnormed = (dq_t * angle_v[0] - swap_rows(dq_t) * angle_v[1]) * unit_v[g]
        for n in range(ALL // WIDTH):
            qsum[...] += dnormed[:, n * WIDTH : (n + 1) * WIDTH]
        dk = jnp.dot(dsbuf[...], query_v[g], preferred_element_type=F32) * scale
        ksum[...] += rows_to_eight(dk * kcos[g])
        lsum[...] += rows_to_eight(dk * ksin[g])
        for at, item in ((g, dk), (KV + g, dv)):
            item = item.astype(BF16)
            ybuf[at, :prompt_rows, :] = item[:prompt_rows]
            ybuf[at, 2 * prompt_rows :, :] = item[prompt_rows:]
        pltpu.make_async_copy(out_ref.at[g], out_hbm.at[g], out_sem.at[g]).start()
        pltpu.make_async_copy(dq_ref.at[g], dq_hbm.at[g], out_sem.at[KV + g]).start()
        return carry

    lax.fori_loop(0, KV, per_kv, 0)

    def mine(back, skip=0):
        return pl.multiple_of(jnp.maximum(rows_of(back, skip), prompt_rows), HALF)

    stores = []
    for n in range(chips):
        for half, target in ((parity, keep_hbm), (1 - parity, send_hbm)):
            start = pl.multiple_of(half * (prompt_rows // 2) + n * share_rows, share_rows)
            stores.append((start, share_rows, target.at[n]))
    stores += [
        (mine(1), LOCAL, swap_hbm.at[:, pl.ds(0, LOCAL), :]),
        (mine(3, LOCAL - HALF), HALF, swap_hbm.at[:, pl.ds(LOCAL, HALF), :]),
        (mine(2), LOCAL, hop_hbm),
        (mine(0), LOCAL, own_hbm),
    ]
    stores = [
        pltpu.make_async_copy(ybuf.at[:, pl.ds(start, size), :], target, out_sem.at[PAIR + n])
        for n, (start, size, target) in enumerate(stores)
    ]
    for store in stores:
        store.start()
    gain_out_ref[0:1, :] = jnp.sum(qsum[...].T, axis=0, keepdims=True)
    second = swap_halves(jnp.sum(lsum[...], axis=0, keepdims=True))
    gain_out_ref[1:2, :] = jnp.sum(ksum[...], axis=0, keepdims=True) + second
    for g in range(KV):
        pltpu.make_async_copy(out_ref.at[g], out_hbm.at[g], out_sem.at[g]).wait()
        pltpu.make_async_copy(dq_ref.at[g], dq_hbm.at[g], out_sem.at[KV + g]).wait()
    for store in stores:
        store.wait()


def finish_kernel(
    gain_ref, angle_hbm, out_t_hbm, dq_t_hbm, unit_hbm, factor_hbm, out_ref, dq_ref, os_, dqs,
    angle_ref, out_t_ref, dq_t_ref, unit_ref, factor_ref, in_sem,
):
    load_all(
        [
            (out_t_hbm, out_t_ref), (dq_t_hbm, dq_t_ref), (unit_hbm, unit_ref), (angle_hbm, angle_ref),
            (factor_hbm, factor_ref),
        ],
        in_sem,
    )
    gain = gain_ref[...]

    def per_kv(g, carry):
        for i in range(BLOCKS):
            span = slice(i * COLS, (i + 1) * COLS)
            out = out_t_ref[g, :, span].astype(F32).T
            dturned = dq_t_ref[g, :, span].astype(F32)
            dnormed = dturned * angle_ref[0, :, span] - swap_rows(dturned) * angle_ref[1, :, span]
            unit = unit_ref[g, :, span]
            dunit = dnormed * gain
            dx = (factor_ref[g, 0:1, span] * (dunit - unit * mean_rows(dunit * unit))).T
            for h in range(GROUP):
                os_[head_rows(i, g, h), :] = out[h * HALF : (h + 1) * HALF]
                dqs[head_rows(i, g, h), :] = dx[h * HALF : (h + 1) * HALF]
        return carry

    lax.fori_loop(0, KV, per_kv, 0)
    out_ref[...] = os_[...].reshape(out_ref.shape).astype(BF16)
    dq_ref[...] = dqs[...].reshape(dq_ref.shape).astype(BF16)


def last_kernel(
    gain_ref, key_ref, own_ref, swap_ref, back_ref, *rest,
):
    blocks, (dk_ref, dv_ref, flat) = rest[:-3], rest[-3:]
    gain = gain_ref[...]
    even = (1 - lax.rem(lax.axis_index("seq"), 2)).astype(F32)

    for ref, first in ((dk_ref, 0), (dv_ref, KV)):
        for g in range(KV):
            at = first + g
            prompt = jnp.concatenate([block[at] for block in blocks], axis=0).astype(F32)
            summed = own_ref[at].astype(F32) + back_ref[at].astype(F32) + prompt
            summed = summed + even * swap_ref[at, :LOCAL].astype(F32)
            if first == 0:
                dnormed = summed * key_ref[0] - swap_halves(summed) * key_ref[1]
                unit = key_ref[2 + g]
                dunit = dnormed * gain
                summed = key_ref[2 + KV + g] * (dunit - unit * mean_lanes(dunit * unit))
            flat[pl.ds(g, LOCAL, stride=KV), :] = summed
        ref[...] = flat[...].reshape(ref.shape).astype(BF16)


def shape(dims, dtype=BF16):
    return jax.ShapeDtypeStruct(dims, dtype)


def cost(flops, size):
    return pl.CostEstimate(flops=flops, bytes_accessed=size, transcendentals=0)


def params(mib):
    return pltpu.CompilerParams(vmem_limit_bytes=mib * 1024 * 1024)


def pack(k, v, share):
    blocks = LOCAL // share
    return pl.pallas_call(
        pack_kernel,
        out_shape=[shape((PAIR, LOCAL, WIDTH))] + [shape((PAIR, share, WIDTH))] * blocks,
        in_specs=[HBM] * 2,
        out_specs=[HBM] * (1 + blocks),
        scratch_shapes=[
            pltpu.VMEM(k.shape, BF16), pltpu.VMEM(k.shape, BF16), pltpu.VMEM((LOCAL * KV, WIDTH), F32),
            pltpu.VMEM((PAIR, LOCAL, WIDTH), BF16),
            pltpu.SemaphoreType.DMA((2,)), pltpu.SemaphoreType.DMA((1 + blocks,)),
        ],
        compiler_params=params(56),
        cost_estimate=cost(1_000_000, 2_000_000),
        name="pack_keys",
    )(k, v)


def prepare(place, rewards, seg, gain, cosine, sine, q, up, k):
    rows = (KV, ALL, WIDTH)
    cols = (KV, WIDTH, ALL)
    shapes = [
        (rows, BF16), (cols, BF16), (rows, BF16), (cols, BF16), (cols, F32), ((KV, 8, ALL), F32),
        ((2, WIDTH, ALL), F32), ((2 + PAIR, LOCAL, WIDTH), F32),
    ]
    return pl.pallas_call(
        prepare_kernel,
        out_shape=[shape(*item) for item in shapes],
        in_specs=[SMEM, SMEM, VMEM, VMEM] + [HBM] * 5,
        out_specs=[HBM] * 8,
        scratch_shapes=[pltpu.VMEM((LOCAL * HEADS, WIDTH), F32)] * 2
        + [pltpu.VMEM(*item) for item in shapes]
        + [pltpu.VMEM(item.shape, item.dtype) for item in (cosine, sine, q, up)]
        + [pltpu.VMEM((KV, LOCAL, WIDTH), BF16), pltpu.SemaphoreType.DMA((5,)), pltpu.SemaphoreType.DMA((8,))],
        compiler_params=params(56),
        cost_estimate=cost(100_000_000, 16_000_000),
        name="prepare_queries",
    )(place, rewards, seg, gain, cosine, sine, q, up, k)


def attend(table, place, gain, cosine, sine, *operands):
    angle, parts = operands[5:7]
    devices, share = 2 * parts.shape[0], parts.shape[2]
    tile_count = devices * LOCAL // TILE
    span_rows = SPAN * TILE
    rows = (KV, ALL, WIDTH)
    cols = (KV, WIDTH, ALL)
    keys = (KV, span_rows, WIDTH)
    keys_t = (KV, WIDTH, span_rows)
    return pl.pallas_call(
        functools.partial(attention_kernel, tile_count),
        out_shape=(
            shape(cols), shape(cols), shape((2, WIDTH), F32),
            shape((devices // 2, PAIR, share, WIDTH)), shape((devices // 2, PAIR, share, WIDTH)),
            shape((PAIR, LOCAL + HALF, WIDTH)), shape((PAIR, LOCAL, WIDTH)), shape((PAIR, LOCAL, WIDTH)),
        ),
        in_specs=[SMEM, SMEM, VMEM] + [HBM] * 13,
        out_specs=(HBM, HBM, VMEM) + (HBM,) * 5,
        scratch_shapes=[
            pltpu.VMEM(cols, BF16), pltpu.VMEM(cols, BF16),
            pltpu.VMEM(cosine.shape, F32), pltpu.VMEM(cosine.shape, F32),
            pltpu.VMEM(rows, BF16), pltpu.VMEM(cols, BF16), pltpu.VMEM(rows, BF16), pltpu.VMEM(cols, BF16),
            pltpu.VMEM(cols, F32), pltpu.VMEM(angle.shape, F32),
            pltpu.VMEM((PAIR, span_rows + PROMPT * TILE, WIDTH), BF16),
            pltpu.VMEM((PAIR, span_rows + PROMPT * TILE, WIDTH), BF16),
            pltpu.VMEM(keys, BF16), pltpu.VMEM(keys_t, BF16), pltpu.VMEM(keys, BF16), pltpu.VMEM(keys_t, BF16),
            pltpu.VMEM(keys, F32), pltpu.VMEM(keys, F32),
            pltpu.VMEM((span_rows, ALL), F32),
            pltpu.VMEM((span_rows, ALL), BF16), pltpu.VMEM((span_rows, ALL), BF16),
            pltpu.VMEM((16, ALL), jnp.int32),
            pltpu.VMEM((8, WIDTH), F32), pltpu.VMEM((8, WIDTH), F32), pltpu.VMEM((WIDTH, WIDTH), F32),
            pltpu.SemaphoreType.DMA((12 + devices,)), pltpu.SemaphoreType.DMA((devices + 4 + PAIR,)),
        ],
        compiler_params=params(56),
        cost_estimate=cost(12 * span_rows * ALL * WIDTH * KV, 12_000_000),
        name="tree_attention",
    )(table, place, gain, cosine, sine, *operands)


def finish(gain, angle, out_t, dq_t, unit, factor):
    dims = (LOCAL, HEADS, WIDTH)
    return pl.pallas_call(
        finish_kernel,
        out_shape=(shape(dims), shape(dims)),
        in_specs=[VMEM] + [HBM] * 5,
        out_specs=(VMEM,) * 2,
        scratch_shapes=[pltpu.VMEM((LOCAL * HEADS, WIDTH), F32)] * 2
        + [pltpu.VMEM(item.shape, item.dtype) for item in (angle, out_t, dq_t, unit, factor)]
        + [pltpu.SemaphoreType.DMA((5,))],
        compiler_params=params(56),
        cost_estimate=cost(100_000_000, 10_000_000),
        name="finish_queries",
    )(gain, angle, out_t, dq_t, unit, factor)


def last(gain, key, own, swap, back, blocks):
    dims = (LOCAL, KV, WIDTH)
    return pl.pallas_call(
        last_kernel,
        out_shape=(shape(dims), shape(dims)),
        in_specs=[VMEM] * (5 + len(blocks)),
        out_specs=(VMEM,) * 2,
        scratch_shapes=[pltpu.VMEM((LOCAL * KV, WIDTH), F32)],
        compiler_params=params(24),
        cost_estimate=cost(1_000_000, 4_000_000),
        name="finish_keys",
    )(gain, key, own, swap, back, *blocks)


def tile_table(tiles, count):
    ids = jnp.arange(count, dtype=jnp.int32)
    row_hits = (tiles[:, 0, None] == ids).astype(jnp.int32) * tiles[:, 2, None]
    col_hits = (tiles[:, 1, None] == ids).astype(jnp.int32)
    table = jnp.einsum("tq,tk->qk", row_hits, col_hits)
    live = (table > 0) & (ids[None, :] >= PROMPT)
    first = jnp.min(jnp.where(live, ids[None, :], count), axis=1)
    inside = (ids >= PROMPT) & (first < count)
    place = jnp.minimum(jnp.where(inside, PROMPT + ids - first, ids), 2 * PROMPT - 1)
    return table.reshape(-1), place


def sum_four(x, axis, step):
    size = lax.axis_size(axis)
    if size <= step:
        return x
    a, b, c = (
        lax.ppermute(x, axis, [(i, i ^ (n * step)) for i in range(size)]) for n in (1, 2, 3)
    )
    return (x + a) + (b + c)


def prompt_pairs(devices, per_owner):
    routes = []
    chips = devices // 2
    for b in range(per_owner):
        pairs = [(owner, owner * per_owner + b) for owner in range(3)]
        routes.append([(owner, 2 * (p % chips) + p // chips) for owner, p in pairs if p < devices])
    return routes


def per_device(q_proj, k_proj, v_proj, upstream, segment_ids, tree_tiles, rewards, q_gain, k_gain):
    devices = lax.axis_size("seq")
    share = PROMPT * TILE // devices
    tile_count = devices * LOCAL // TILE
    routes = prompt_pairs(devices, LOCAL // share)
    even = lax.rem(lax.axis_index("seq"), 2) == 0
    cores = [(i, i ^ 1) for i in range(devices)]

    kv, *blocks = pack(k_proj[0], v_proj[0], share)
    mine = [lax.ppermute(block, "seq", pairs) for block, pairs in zip(blocks, routes)]
    hop_in = lax.ppermute(kv, "seq", [(i, i + 2) for i in range(devices - 2)])
    mine = mine[0] + mine[1] + mine[2] + mine[3] + mine[4] + mine[5]
    mine, hop_in = lax.optimization_barrier((mine, hop_in))
    chips = devices // 2
    parities = [list(range(j, devices, 2)) for j in range(2)]

    def exchange(x):
        return lax.all_to_all(x, "seq", split_axis=0, concat_axis=0, tiled=True, axis_index_groups=parities)

    parts = exchange(jnp.broadcast_to(mine[None], (chips,) + mine.shape))
    swap_in = jnp.where(
        even,
        jnp.concatenate([kv, hop_in[:, LOCAL - HALF :]], axis=1),
        jnp.concatenate([hop_in, hop_in[:, LOCAL - HALF :]], axis=1),
    )
    swap_in = lax.ppermute(swap_in, "seq", cores)

    table, place = tile_table(tree_tiles[0], tile_count)
    cosine, sine = (jnp.asarray(item) for item in rope_tables(2 * PROMPT * TILE))
    query, query_t, grad, grad_t, unit, factor, angle, own_key = prepare(
        place, rewards[0], segment_ids, q_gain[:, None], cosine, sine, q_proj[0], upstream[0],
        kv,
    )
    parts, swap_in, query = lax.optimization_barrier((parts, swap_in, query))
    others = lax.ppermute(parts, "seq", cores)
    out_t, dq_t, gains, keep, send, swap, hop, own = attend(
        table, place, k_gain[None], cosine, sine, query, query_t, grad, grad_t, unit, angle,
        parts, others, kv, hop_in, swap_in,
    )

    got = lax.ppermute(send, "seq", cores)
    parts = exchange(keep + got)
    swap = lax.ppermute(swap, "seq", cores)
    far = jnp.concatenate([jnp.zeros((PAIR, LOCAL - HALF, WIDTH), BF16), swap[:, LOCAL:]], axis=1)
    hop = hop + jnp.where(even, far, swap[:, :LOCAL])
    back = lax.ppermute(hop, "seq", [(i, i - 2) for i in range(2, devices)])
    gains = sum_four(gains, "dp", 1)
    gains, out_t, dq_t = lax.optimization_barrier((gains, out_t, dq_t))
    out, dq = finish(q_gain[:, None], angle, out_t, dq_t, unit, factor)
    gains = sum_four(sum_four(gains, "dp", 4), "seq", 1)
    piece = jnp.sum(parts.astype(F32), axis=0).astype(BF16)
    piece, gains, out, dq = lax.optimization_barrier((piece, gains, out, dq))
    blocks = [lax.ppermute(piece, "seq", [(b, a) for a, b in pairs]) for pairs in routes]
    gains = sum_four(gains, "seq", 4)
    dk, dv = last(k_gain[None], own_key, own, swap, back, blocks)
    return (out[None], dq[None], dk[None], dv[None], gains[0], gains[1])


def solution(mesh):
    whole = P("dp", "seq", None, None)
    return jax.shard_map(
        per_device,
        mesh=mesh,
        in_specs=(whole, whole, whole, whole, P("dp", "seq"), P("dp", None, None), P("dp", None), P(), P()),
        out_specs=(whole, whole, whole, whole, P(), P()),
        check_vma=False,
    )
```

```python
import functools
import math

import jax
import jax.numpy as jnp
import numpy as np
from jax import lax
from jax.experimental import pallas as pl
from jax.experimental.pallas import tpu as pltpu
from jax.sharding import PartitionSpec as P

TILE = 128
PROMPT = 4
WINDOW = 5
SPAN = PROMPT + WINDOW
RESPONSES = 5
HEADS = 16
KV = 4
GROUP = HEADS // KV
WIDTH = 128
HALF = 64
BLOCKS = 3
COLS = GROUP * HALF
ALL = BLOCKS * COLS
LOCAL = BLOCKS * HALF
PAIR = 2 * KV
EPS = 1e-06
ROPE_BASE = 1000000.0
F32 = jnp.float32
BF16 = jnp.bfloat16
VMEM = pl.BlockSpec(memory_space=pltpu.VMEM)
SMEM = pl.BlockSpec(memory_space=pltpu.SMEM)
HBM = pl.BlockSpec(memory_space=pltpu.HBM)


def rope_tables(count):
    freq = np.exp(
        np.arange(WIDTH // 2, dtype=np.float32) * np.float32(-2.0 * math.log(ROPE_BASE) / WIDTH)
    ).astype(np.float32)
    angle = (np.arange(count, dtype=np.float32)[:, None] * freq[None, :]).astype(np.float64)
    cosine, sine = np.cos(angle), np.sin(angle)
    return (
        np.concatenate([cosine, cosine], axis=1).astype(np.float32),
        np.concatenate([-sine, sine], axis=1).astype(np.float32),
    )


def swap_halves(x):
    return pltpu.roll(x, WIDTH // 2, 1)


def mean_lanes(x):
    return jnp.sum(x, axis=1, keepdims=True) * (1.0 / WIDTH)


def rows_to_eight(x):
    return jnp.sum(x.reshape(-1, 8, WIDTH), axis=0)


def head_rows(i, g, h):
    return pl.ds(i * HALF * HEADS + GROUP * g + h, HALF, stride=HEADS)


def swap_rows(x):
    return jnp.concatenate([x[WIDTH // 2 :], x[: WIDTH // 2]], axis=0)


def mean_rows(x):
    return jnp.sum(x, axis=0, keepdims=True) * (1.0 / WIDTH)


def pack_kernel(k_hbm, v_hbm, kv_hbm, *rest):
    targets, (k_ref, v_ref, flat, kv_ref, in_sem, out_sem) = rest[:-6], rest[-6:]
    loads = [
        pltpu.make_async_copy(k_hbm, k_ref, in_sem.at[0]),
        pltpu.make_async_copy(v_hbm, v_ref, in_sem.at[1]),
    ]
    for load in loads:
        load.start()
    for n, ref in enumerate((k_ref, v_ref)):
        loads[n].wait()
        flat[...] = ref[...].astype(F32).reshape(flat.shape)
        for g in range(KV):
            kv_ref[n * KV + g] = flat[pl.ds(g, LOCAL, stride=KV), :].astype(BF16)
    stores = [pltpu.make_async_copy(kv_ref, kv_hbm, out_sem.at[0])]
    for b, target in enumerate(targets):
        size = target.shape[1]
        stores.append(
            pltpu.make_async_copy(kv_ref.at[:, pl.ds(b * size, size), :], target, out_sem.at[1 + b])
        )
    for store in stores:
        store.start()
    for store in stores:
        store.wait()


def load_all(pairs, sems):
    loads = [pltpu.make_async_copy(a, b, sems.at[n]) for n, (a, b) in enumerate(pairs)]
    for load in loads:
        load.start()
    for load in loads:
        load.wait()


def prepare_kernel(
    place_ref, rewards_ref, seg_ref, gain_ref, cos_hbm, sin_hbm, q_hbm, up_hbm, k_hbm,
    query_hbm, query_t_hbm, grad_hbm, grad_t_hbm, unit_hbm, factor_hbm, angle_hbm, own_hbm, xq, xu,
    query_ref, query_t_ref, grad_ref, grad_t_ref, unit_ref, factor_ref, angle_ref, own_ref,
    cos_ref, sin_ref, q_ref, up_ref, k_ref, in_sem, out_sem,
):
    load_all(
        [(q_hbm, q_ref), (up_hbm, up_ref), (cos_hbm, cos_ref), (sin_hbm, sin_ref), (k_hbm.at[pl.ds(0, KV)], k_ref)],
        in_sem,
    )
    xq[...] = q_ref[...].astype(F32).reshape(xq.shape)
    xu[...] = up_ref[...].astype(F32).reshape(xu.shape)
    gain = gain_ref[...]
    reward = [rewards_ref[r] for r in range(RESPONSES)]
    centre = (reward[0] + reward[1] + reward[2] + reward[3] + reward[4]) * (1.0 / RESPONSES)
    seg = seg_ref[...]
    adv_row = jnp.zeros(seg.shape, F32)
    for r in range(RESPONSES):
        adv_row = adv_row + jnp.where(seg == r + 1, reward[r] - centre, 0.0)
    for i in range(BLOCKS):
        block = BLOCKS * lax.axis_index("seq") + i
        start = place_ref[block // 2] * TILE + lax.rem(block, 2) * HALF
        start = pl.multiple_of(start, HALF)
        for n, ref in enumerate((cos_ref, sin_ref)):
            angle = ref[pl.ds(start, HALF), :]
            angle_ref[n, :, i * COLS : (i + 1) * COLS] = jnp.concatenate([angle] * GROUP, axis=0).T
            own_ref[n, i * HALF : (i + 1) * HALF, :] = angle
    for g in range(KV):
        x = k_ref[g].astype(F32)
        factor = lax.rsqrt(mean_lanes(x * x) + EPS)
        own_ref[2 + g] = x * factor
        own_ref[2 + KV + g] = jnp.broadcast_to(factor, (LOCAL, WIDTH))

    def per_kv(g, carry):
        for i in range(BLOCKS):
            span = slice(i * COLS, (i + 1) * COLS)

            def columns(ref):
                rows = [ref[head_rows(i, g, h), :] for h in range(GROUP)]
                return jnp.concatenate(rows, axis=0).T

            x = columns(xq)
            factor = lax.rsqrt(mean_rows(x * x) + EPS)
            unit = x * factor
            normed = unit * gain
            turned = normed * angle_ref[0, :, span] + swap_rows(normed) * angle_ref[1, :, span]
            query_ref[g, span, :] = turned.T.astype(BF16)
            query_t_ref[g, :, span] = turned.astype(BF16)
            unit_ref[g, :, span] = unit
            factor_ref[g, :, span] = jnp.broadcast_to(factor, (8, COLS))
            adv = jnp.concatenate([adv_row[:, i * HALF : (i + 1) * HALF]] * GROUP, axis=1)
            grad = columns(xu) * adv
            grad_t_ref[g, :, span] = grad.astype(BF16)
            grad_ref[g, span, :] = grad.T.astype(BF16)
        return carry

    lax.fori_loop(0, KV, per_kv, 0)
    stores = [
        pltpu.make_async_copy(source, target, out_sem.at[n])
        for n, (source, target) in enumerate(
            [
                (query_ref, query_hbm), (query_t_ref, query_t_hbm), (grad_ref, grad_hbm),
                (grad_t_ref, grad_t_hbm), (unit_ref, unit_hbm), (factor_ref, factor_hbm),
                (angle_ref, angle_hbm), (own_ref, own_hbm),
            ]
        )
    ]
    for store in stores:
        store.start()
    for store in stores:
        store.wait()


def attention_kernel(
    tile_count, table_ref, place_ref, gain_ref, cos_hbm, sin_hbm,
    query_hbm, query_t_hbm, grad_hbm, grad_t_hbm, unit_hbm, angle_hbm,
    parts_hbm, others_hbm, mine_hbm, hop_in_hbm, swap_in_hbm,
    out_hbm, dq_hbm, gain_out_ref, keep_hbm, send_hbm, swap_hbm, hop_hbm, own_hbm,
    out_ref, dq_ref, cos_ref, sin_ref, query_v, query_t_v, grad_v, grad_t_v, unit_v, angle_v,
    kvb, ybuf, kr, kt, vr, vt, kcos, ksin, ebuf, pbuf, dsbuf, limits, ksum, lsum, qsum,
    in_sem, out_sem,
):
    me = lax.axis_index("seq")
    wb = jnp.clip((BLOCKS * me) // 2 - 3, PROMPT, tile_count - WINDOW)
    prompt_rows = PROMPT * TILE

    def rows_of(back, skip=0):
        return pl.multiple_of((me - back) * LOCAL + skip - wb * TILE + 2 * prompt_rows, HALF)

    kvb[:, 2 * prompt_rows :, :] = jnp.zeros((PAIR, WINDOW * TILE, WIDTH), BF16)
    chips, _, share_rows, _ = parts_hbm.shape
    devices = 2 * chips
    parity = lax.rem(me, 2)
    key_loads = []
    for n in range(chips):
        for at, half, source in ((2 * n, parity, parts_hbm), (2 * n + 1, 1 - parity, others_hbm)):
            start = pl.multiple_of(half * (prompt_rows // 2) + n * share_rows, share_rows)
            target = kvb.at[:, pl.ds(start, share_rows), :]
            key_loads.append(pltpu.make_async_copy(source.at[n], target, in_sem.at[8 + at]))
    key_loads.append(pltpu.make_async_copy(cos_hbm, cos_ref, in_sem.at[6]))
    key_loads.append(pltpu.make_async_copy(sin_hbm, sin_ref, in_sem.at[7]))
    window_loads = [
        (0, pltpu.make_async_copy(mine_hbm, kvb.at[:, pl.ds(rows_of(0), LOCAL), :], in_sem.at[8 + devices]))
    ]

    def earlier(back, source, skip, size):
        start = jnp.maximum(rows_of(back, skip), prompt_rows)
        target = kvb.at[:, pl.ds(pl.multiple_of(start, HALF), size), :]
        window_loads.append((back, pltpu.make_async_copy(source, target, in_sem.at[8 + devices + back])))

    earlier(1, swap_in_hbm.at[:, pl.ds(0, LOCAL), :], 0, LOCAL)
    earlier(2, hop_in_hbm, 0, LOCAL)
    earlier(3, swap_in_hbm.at[:, pl.ds(LOCAL, HALF), :], LOCAL - HALF, HALF)
    loads = [
        pltpu.make_async_copy(query_t_hbm, query_t_v, in_sem.at[0]),
        pltpu.make_async_copy(grad_t_hbm, grad_t_v, in_sem.at[1]),
        pltpu.make_async_copy(query_hbm, query_v, in_sem.at[2]),
        pltpu.make_async_copy(grad_hbm, grad_v, in_sem.at[3]),
        pltpu.make_async_copy(unit_hbm, unit_v, in_sem.at[4]),
        pltpu.make_async_copy(angle_hbm, angle_v, in_sem.at[5]),
    ]
    for load in key_loads:
        load.start()
    for back, load in window_loads:
        pl.when(me >= back)(load.start)

    gain = gain_ref[...]
    gain_turned = swap_halves(gain)
    ksum[...] = jnp.zeros_like(ksum)
    lsum[...] = jnp.zeros_like(lsum)
    qsum[...] = jnp.zeros_like(qsum)
    ybuf[:, prompt_rows : 2 * prompt_rows] = jnp.zeros((PAIR, prompt_rows, WIDTH), BF16)

    lane = lax.broadcasted_iota(jnp.int32, (1, COLS), 1)
    key_place = [tile * TILE for tile in range(PROMPT)]
    key_place += [pl.multiple_of(place_ref[wb + j] * TILE, TILE) for j in range(WINDOW)]
    for tile in range(SPAN):
        name = tile if tile < PROMPT else wb + tile - PROMPT
        for i in range(BLOCKS):
            block = BLOCKS * me + i
            kind = table_ref[(block // 2) * tile_count + name]
            one = (kind == 1).astype(jnp.int32)
            two = (kind == 2).astype(jnp.int32)
            slot = lax.rem(block, 2) * HALF + lax.rem(lane, HALF)
            limits[tile : tile + 1, i * COLS : (i + 1) * COLS] = (
                two * slot + (one * (TILE + 1) - 1 + two)
            )

    for load in key_loads:
        load.wait()
    for back, load in window_loads:
        pl.when(me >= back)(load.wait)
    for load in loads:
        load.start()

    def prepare_keys(g, carry):
        for tile in range(SPAN):
            at = slice(tile * TILE, (tile + 1) * TILE)
            source = tile * TILE if tile < PROMPT else tile * TILE + prompt_rows
            source = slice(source, source + TILE)
            x = kvb[g, source, :].astype(F32)
            factor = lax.rsqrt(mean_lanes(x * x) + EPS)
            unit = x * factor
            first = unit * cos_ref[pl.ds(key_place[tile], TILE), :]
            second = swap_halves(unit) * sin_ref[pl.ds(key_place[tile], TILE), :]
            turned = first * gain + second * gain_turned
            kcos[g, at, :] = first
            ksin[g, at, :] = second
            kr[g, at, :] = turned.astype(BF16)
            kt[g, :, at] = turned.T.astype(BF16)
            value = kvb[KV + g, source, :]
            vr[g, at, :] = value
            vt[g, :, at] = value.astype(F32).T.astype(BF16)
        return carry

    lax.fori_loop(0, KV, prepare_keys, 0)
    for load in loads:
        load.wait()

    scale = 1.0 / math.sqrt(WIDTH)
    key_at = lax.broadcasted_iota(jnp.int32, (TILE, ALL), 0)
    third = SPAN // 3

    def per_kv(g, carry):
        query_t = query_t_v[g]
        grad_t = grad_t_v[g]
        total = jnp.zeros((1, ALL), F32)
        for c in range(3):
            rows = slice(c * third * TILE, (c + 1) * third * TILE)
            score = jnp.dot(kr[g, rows, :], query_t, preferred_element_type=F32)
            for t in range(third):
                tile = c * third + t
                raw = jnp.where(
                    key_at <= limits[tile : tile + 1, :],
                    jnp.exp2(score[t * TILE : (t + 1) * TILE] * (scale * math.log2(math.e))),
                    0.0,
                )
                ebuf[tile * TILE : (tile + 1) * TILE, :] = raw
                total = total + jnp.sum(raw, axis=0, keepdims=True)
        share = jnp.where(total > 0, 1.0 / total, 0.0)
        for tile in range(SPAN):
            at = slice(tile * TILE, (tile + 1) * TILE)
            pbuf[at, :] = (ebuf[at, :] * share).astype(BF16)
        out_t = jnp.dot(vt[g], pbuf[...], preferred_element_type=F32)
        out_ref[g] = out_t.astype(BF16)
        delta = jnp.sum(grad_t.astype(F32) * out_t, axis=0, keepdims=True)
        for c in range(3):
            rows = slice(c * third * TILE, (c + 1) * third * TILE)
            dweights = jnp.dot(vr[g, rows, :], grad_t, preferred_element_type=F32)
            dsbuf[rows, :] = (
                pbuf[rows, :].astype(F32) * (dweights - delta)
            ).astype(BF16)
        dv = jnp.dot(pbuf[...], grad_v[g], preferred_element_type=F32)
        dq_t = jnp.dot(kt[g], dsbuf[...], preferred_element_type=F32)
        dq_t = (dq_t * scale).astype(BF16)
        dq_ref[g] = dq_t
        dq_t = dq_t.astype(F32)
        dnormed = (dq_t * angle_v[0] - swap_rows(dq_t) * angle_v[1]) * unit_v[g]
        for n in range(ALL // WIDTH):
            qsum[...] += dnormed[:, n * WIDTH : (n + 1) * WIDTH]
        dk = jnp.dot(dsbuf[...], query_v[g], preferred_element_type=F32) * scale
        ksum[...] += rows_to_eight(dk * kcos[g])
        lsum[...] += rows_to_eight(dk * ksin[g])
        for at, item in ((g, dk), (KV + g, dv)):
            item = item.astype(BF16)
            ybuf[at, :prompt_rows, :] = item[:prompt_rows]
            ybuf[at, 2 * prompt_rows :, :] = item[prompt_rows:]
        pltpu.make_async_copy(out_ref.at[g], out_hbm.at[g], out_sem.at[g]).start()
        pltpu.make_async_copy(dq_ref.at[g], dq_hbm.at[g], out_sem.at[KV + g]).start()
        return carry

    lax.fori_loop(0, KV, per_kv, 0)

    def mine(back, skip=0):
        return pl.multiple_of(jnp.maximum(rows_of(back, skip), prompt_rows), HALF)

    stores = []
    for n in range(chips):
        for half, target in ((parity, keep_hbm), (1 - parity, send_hbm)):
            start = pl.multiple_of(half * (prompt_rows // 2) + n * share_rows, share_rows)
            stores.append((start, share_rows, target.at[n]))
    stores += [
        (mine(1), LOCAL, swap_hbm.at[:, pl.ds(0, LOCAL), :]),
        (mine(3, LOCAL - HALF), HALF, swap_hbm.at[:, pl.ds(LOCAL, HALF), :]),
        (mine(2), LOCAL, hop_hbm),
        (mine(0), LOCAL, own_hbm),
    ]
    stores = [
        pltpu.make_async_copy(ybuf.at[:, pl.ds(start, size), :], target, out_sem.at[PAIR + n])
        for n, (start, size, target) in enumerate(stores)
    ]
    for store in stores:
        store.start()
    gain_out_ref[0:1, :] = jnp.sum(qsum[...].T, axis=0, keepdims=True)
    second = swap_halves(jnp.sum(lsum[...], axis=0, keepdims=True))
    gain_out_ref[1:2, :] = jnp.sum(ksum[...], axis=0, keepdims=True) + second
    for g in range(KV):
        pltpu.make_async_copy(out_ref.at[g], out_hbm.at[g], out_sem.at[g]).wait()
        pltpu.make_async_copy(dq_ref.at[g], dq_hbm.at[g], out_sem.at[KV + g]).wait()
    for store in stores:
        store.wait()


def finish_kernel(
    gain_ref, angle_hbm, out_t_hbm, dq_t_hbm, unit_hbm, factor_hbm, out_ref, dq_ref, os_, dqs,
    angle_ref, out_t_ref, dq_t_ref, unit_ref, factor_ref, in_sem,
):
    load_all(
        [
            (out_t_hbm, out_t_ref), (dq_t_hbm, dq_t_ref), (unit_hbm, unit_ref), (angle_hbm, angle_ref),
            (factor_hbm, factor_ref),
        ],
        in_sem,
    )
    gain = gain_ref[...]

    def per_kv(g, carry):
        for i in range(BLOCKS):
            span = slice(i * COLS, (i + 1) * COLS)
            out = out_t_ref[g, :, span].astype(F32).T
            dturned = dq_t_ref[g, :, span].astype(F32)
            dnormed = dturned * angle_ref[0, :, span] - swap_rows(dturned) * angle_ref[1, :, span]
            unit = unit_ref[g, :, span]
            dunit = dnormed * gain
            dx = (factor_ref[g, 0:1, span] * (dunit - unit * mean_rows(dunit * unit))).T
            for h in range(GROUP):
                os_[head_rows(i, g, h), :] = out[h * HALF : (h + 1) * HALF]
                dqs[head_rows(i, g, h), :] = dx[h * HALF : (h + 1) * HALF]
        return carry

    lax.fori_loop(0, KV, per_kv, 0)
    out_ref[...] = os_[...].reshape(out_ref.shape).astype(BF16)
    dq_ref[...] = dqs[...].reshape(dq_ref.shape).astype(BF16)


def last_kernel(
    gain_ref, key_ref, own_ref, swap_ref, back_ref, *rest,
):
    blocks, (dk_ref, dv_ref, flat) = rest[:-3], rest[-3:]
    gain = gain_ref[...]
    even = (1 - lax.rem(lax.axis_index("seq"), 2)).astype(F32)

    for ref, first in ((dk_ref, 0), (dv_ref, KV)):
        for g in range(KV):
            at = first + g
            prompt = jnp.concatenate([block[at] for block in blocks], axis=0).astype(F32)
            summed = own_ref[at].astype(F32) + back_ref[at].astype(F32) + prompt
            summed = summed + even * swap_ref[at, :LOCAL].astype(F32)
            if first == 0:
                dnormed = summed * key_ref[0] - swap_halves(summed) * key_ref[1]
                unit = key_ref[2 + g]
                dunit = dnormed * gain
                summed = key_ref[2 + KV + g] * (dunit - unit * mean_lanes(dunit * unit))
            flat[pl.ds(g, LOCAL, stride=KV), :] = summed
        ref[...] = flat[...].reshape(ref.shape).astype(BF16)


def shape(dims, dtype=BF16):
    return jax.ShapeDtypeStruct(dims, dtype)


def cost(flops, size):
    return pl.CostEstimate(flops=flops, bytes_accessed=size, transcendentals=0)


def params(mib):
    return pltpu.CompilerParams(vmem_limit_bytes=mib * 1024 * 1024)


def pack(k, v, share):
    blocks = LOCAL // share
    return pl.pallas_call(
        pack_kernel,
        out_shape=[shape((PAIR, LOCAL, WIDTH))] + [shape((PAIR, share, WIDTH))] * blocks,
        in_specs=[HBM] * 2,
        out_specs=[HBM] * (1 + blocks),
        scratch_shapes=[
            pltpu.VMEM(k.shape, BF16), pltpu.VMEM(k.shape, BF16), pltpu.VMEM((LOCAL * KV, WIDTH), F32),
            pltpu.VMEM((PAIR, LOCAL, WIDTH), BF16),
            pltpu.SemaphoreType.DMA((2,)), pltpu.SemaphoreType.DMA((1 + blocks,)),
        ],
        compiler_params=params(56),
        cost_estimate=cost(1_000_000, 2_000_000),
        name="pack_keys",
    )(k, v)


def prepare(place, rewards, seg, gain, cosine, sine, q, up, k):
    rows = (KV, ALL, WIDTH)
    cols = (KV, WIDTH, ALL)
    shapes = [
        (rows, BF16), (cols, BF16), (rows, BF16), (cols, BF16), (cols, F32), ((KV, 8, ALL), F32),
        ((2, WIDTH, ALL), F32), ((2 + PAIR, LOCAL, WIDTH), F32),
    ]
    return pl.pallas_call(
        prepare_kernel,
        out_shape=[shape(*item) for item in shapes],
        in_specs=[SMEM, SMEM, VMEM, VMEM] + [HBM] * 5,
        out_specs=[HBM] * 8,
        scratch_shapes=[pltpu.VMEM((LOCAL * HEADS, WIDTH), F32)] * 2
        + [pltpu.VMEM(*item) for item in shapes]
        + [pltpu.VMEM(item.shape, item.dtype) for item in (cosine, sine, q, up)]
        + [pltpu.VMEM((KV, LOCAL, WIDTH), BF16), pltpu.SemaphoreType.DMA((5,)), pltpu.SemaphoreType.DMA((8,))],
        compiler_params=params(56),
        cost_estimate=cost(100_000_000, 16_000_000),
        name="prepare_queries",
    )(place, rewards, seg, gain, cosine, sine, q, up, k)


def attend(table, place, gain, cosine, sine, *operands):
    angle, parts = operands[5:7]
    devices, share = 2 * parts.shape[0], parts.shape[2]
    tile_count = devices * LOCAL // TILE
    span_rows = SPAN * TILE
    rows = (KV, ALL, WIDTH)
    cols = (KV, WIDTH, ALL)
    keys = (KV, span_rows, WIDTH)
    keys_t = (KV, WIDTH, span_rows)
    return pl.pallas_call(
        functools.partial(attention_kernel, tile_count),
        out_shape=(
            shape(cols), shape(cols), shape((2, WIDTH), F32),
            shape((devices // 2, PAIR, share, WIDTH)), shape((devices // 2, PAIR, share, WIDTH)),
            shape((PAIR, LOCAL + HALF, WIDTH)), shape((PAIR, LOCAL, WIDTH)), shape((PAIR, LOCAL, WIDTH)),
        ),
        in_specs=[SMEM, SMEM, VMEM] + [HBM] * 13,
        out_specs=(HBM, HBM, VMEM) + (HBM,) * 5,
        scratch_shapes=[
            pltpu.VMEM(cols, BF16), pltpu.VMEM(cols, BF16),
            pltpu.VMEM(cosine.shape, F32), pltpu.VMEM(cosine.shape, F32),
            pltpu.VMEM(rows, BF16), pltpu.VMEM(cols, BF16), pltpu.VMEM(rows, BF16), pltpu.VMEM(cols, BF16),
            pltpu.VMEM(cols, F32), pltpu.VMEM(angle.shape, F32),
            pltpu.VMEM((PAIR, span_rows + PROMPT * TILE, WIDTH), BF16),
            pltpu.VMEM((PAIR, span_rows + PROMPT * TILE, WIDTH), BF16),
            pltpu.VMEM(keys, BF16), pltpu.VMEM(keys_t, BF16), pltpu.VMEM(keys, BF16), pltpu.VMEM(keys_t, BF16),
            pltpu.VMEM(keys, F32), pltpu.VMEM(keys, F32),
            pltpu.VMEM((span_rows, ALL), F32),
            pltpu.VMEM((span_rows, ALL), BF16), pltpu.VMEM((span_rows, ALL), BF16),
            pltpu.VMEM((16, ALL), jnp.int32),
            pltpu.VMEM((8, WIDTH), F32), pltpu.VMEM((8, WIDTH), F32), pltpu.VMEM((WIDTH, WIDTH), F32),
            pltpu.SemaphoreType.DMA((12 + devices,)), pltpu.SemaphoreType.DMA((devices + 4 + PAIR,)),
        ],
        compiler_params=params(56),
        cost_estimate=cost(12 * span_rows * ALL * WIDTH * KV, 12_000_000),
        name="tree_attention",
    )(table, place, gain, cosine, sine, *operands)


def finish(gain, angle, out_t, dq_t, unit, factor):
    dims = (LOCAL, HEADS, WIDTH)
    return pl.pallas_call(
        finish_kernel,
        out_shape=(shape(dims), shape(dims)),
        in_specs=[VMEM] + [HBM] * 5,
        out_specs=(VMEM,) * 2,
        scratch_shapes=[pltpu.VMEM((LOCAL * HEADS, WIDTH), F32)] * 2
        + [pltpu.VMEM(item.shape, item.dtype) for item in (angle, out_t, dq_t, unit, factor)]
        + [pltpu.SemaphoreType.DMA((5,))],
        compiler_params=params(56),
        cost_estimate=cost(100_000_000, 10_000_000),
        name="finish_queries",
    )(gain, angle, out_t, dq_t, unit, factor)


def last(gain, key, own, swap, back, blocks):
    dims = (LOCAL, KV, WIDTH)
    return pl.pallas_call(
        last_kernel,
        out_shape=(shape(dims), shape(dims)),
        in_specs=[VMEM] * (5 + len(blocks)),
        out_specs=(VMEM,) * 2,
        scratch_shapes=[pltpu.VMEM((LOCAL * KV, WIDTH), F32)],
        compiler_params=params(24),
        cost_estimate=cost(1_000_000, 4_000_000),
        name="finish_keys",
    )(gain, key, own, swap, back, *blocks)


def tile_table(tiles, count):
    ids = jnp.arange(count, dtype=jnp.int32)
    row_hits = (tiles[:, 0, None] == ids).astype(jnp.int32) * tiles[:, 2, None]
    col_hits = (tiles[:, 1, None] == ids).astype(jnp.int32)
    table = jnp.einsum("tq,tk->qk", row_hits, col_hits)
    live = (table > 0) & (ids[None, :] >= PROMPT)
    first = jnp.min(jnp.where(live, ids[None, :], count), axis=1)
    inside = (ids >= PROMPT) & (first < count)
    place = jnp.minimum(jnp.where(inside, PROMPT + ids - first, ids), 2 * PROMPT - 1)
    return table.reshape(-1), place


def sum_four(x, axis, step):
    size = lax.axis_size(axis)
    if size <= step:
        return x
    a, b, c = (
        lax.ppermute(x, axis, [(i, i ^ (n * step)) for i in range(size)]) for n in (1, 2, 3)
    )
    return (x + a) + (b + c)


def prompt_pairs(devices, per_owner):
    routes = []
    chips = devices // 2
    for b in range(per_owner):
        pairs = [(owner, owner * per_owner + b) for owner in range(3)]
        routes.append([(owner, 2 * (p % chips) + p // chips) for owner, p in pairs if p < devices])
    return routes


def per_device(q_proj, k_proj, v_proj, upstream, segment_ids, tree_tiles, rewards, q_gain, k_gain):
    devices = lax.axis_size("seq")
    share = PROMPT * TILE // devices
    tile_count = devices * LOCAL // TILE
    routes = prompt_pairs(devices, LOCAL // share)
    even = lax.rem(lax.axis_index("seq"), 2) == 0
    cores = [(i, i ^ 1) for i in range(devices)]

    kv, *blocks = pack(k_proj[0], v_proj[0], share)
    mine = [lax.ppermute(block, "seq", pairs) for block, pairs in zip(blocks, routes)]
    hop_in = lax.ppermute(kv, "seq", [(i, i + 2) for i in range(devices - 2)])
    mine = mine[0] + mine[1] + mine[2] + mine[3] + mine[4] + mine[5]
    mine, hop_in = lax.optimization_barrier((mine, hop_in))
    chips = devices // 2
    parities = [list(range(j, devices, 2)) for j in range(2)]

    def exchange(x):
        return lax.all_to_all(x, "seq", split_axis=0, concat_axis=0, tiled=True, axis_index_groups=parities)

    parts = exchange(jnp.broadcast_to(mine[None], (chips,) + mine.shape))
    swap_in = jnp.where(
        even,
        jnp.concatenate([kv, hop_in[:, LOCAL - HALF :]], axis=1),
        jnp.concatenate([hop_in, hop_in[:, LOCAL - HALF :]], axis=1),
    )
    swap_in = lax.ppermute(swap_in, "seq", cores)

    table, place = tile_table(tree_tiles[0], tile_count)
    cosine, sine = (jnp.asarray(item) for item in rope_tables(2 * PROMPT * TILE))
    query, query_t, grad, grad_t, unit, factor, angle, own_key = prepare(
        place, rewards[0], segment_ids, q_gain[:, None], cosine, sine, q_proj[0], upstream[0],
        kv,
    )
    parts, swap_in, query = lax.optimization_barrier((parts, swap_in, query))
    others = lax.ppermute(parts, "seq", cores)
    out_t, dq_t, gains, keep, send, swap, hop, own = attend(
        table, place, k_gain[None], cosine, sine, query, query_t, grad, grad_t, unit, angle,
        parts, others, kv, hop_in, swap_in,
    )

    got = lax.ppermute(send, "seq", cores)
    parts = exchange(keep + got)
    swap = lax.ppermute(swap, "seq", cores)
    far = jnp.concatenate([jnp.zeros((PAIR, LOCAL - HALF, WIDTH), BF16), swap[:, LOCAL:]], axis=1)
    hop = hop + jnp.where(even, far, swap[:, :LOCAL])
    back = lax.ppermute(hop, "seq", [(i, i - 2) for i in range(2, devices)])
    gains = sum_four(gains, "dp", 1)
    gains, out_t, dq_t = lax.optimization_barrier((gains, out_t, dq_t))
    out, dq = finish(q_gain[:, None], angle, out_t, dq_t, unit, factor)
    gains = sum_four(sum_four(gains, "dp", 4), "seq", 4)
    piece = jnp.sum(parts.astype(F32), axis=0).astype(BF16)
    piece, gains, out, dq = lax.optimization_barrier((piece, gains, out, dq))
    blocks = [lax.ppermute(piece, "seq", [(b, a) for a, b in pairs]) for pairs in routes]
    gains = sum_four(gains, "seq", 1)
    dk, dv = last(k_gain[None], own_key, own, swap, back, blocks)
    return (out[None], dq[None], dk[None], dv[None], gains[0], gains[1])


def solution(mesh):
    whole = P("dp", "seq", None, None)
    return jax.shard_map(
        per_device,
        mesh=mesh,
        in_specs=(whole, whole, whole, whole, P("dp", "seq"), P("dp", None, None), P("dp", None), P(), P()),
        out_specs=(whole, whole, whole, whole, P(), P()),
        check_vma=False,
    )
```

```python
import functools
import math

import jax
import jax.numpy as jnp
import numpy as np
from jax import lax
from jax.experimental import pallas as pl
from jax.experimental.pallas import tpu as pltpu
from jax.sharding import PartitionSpec as P

TILE = 128
PROMPT = 4
WINDOW = 5
SPAN = PROMPT + WINDOW
RESPONSES = 5
HEADS = 16
KV = 4
GROUP = HEADS // KV
WIDTH = 128
HALF = 64
BLOCKS = 3
COLS = GROUP * HALF
ALL = BLOCKS * COLS
LOCAL = BLOCKS * HALF
PAIR = 2 * KV
EPS = 1e-06
ROPE_BASE = 1000000.0
F32 = jnp.float32
BF16 = jnp.bfloat16
VMEM = pl.BlockSpec(memory_space=pltpu.VMEM)
SMEM = pl.BlockSpec(memory_space=pltpu.SMEM)
HBM = pl.BlockSpec(memory_space=pltpu.HBM)


def rope_tables(count):
    freq = np.exp(
        np.arange(WIDTH // 2, dtype=np.float32) * np.float32(-2.0 * math.log(ROPE_BASE) / WIDTH)
    ).astype(np.float32)
    angle = (np.arange(count, dtype=np.float32)[:, None] * freq[None, :]).astype(np.float64)
    cosine, sine = np.cos(angle), np.sin(angle)
    return (
        np.concatenate([cosine, cosine], axis=1).astype(np.float32),
        np.concatenate([-sine, sine], axis=1).astype(np.float32),
    )


def swap_halves(x):
    return pltpu.roll(x, WIDTH // 2, 1)


def mean_lanes(x):
    return jnp.sum(x, axis=1, keepdims=True) * (1.0 / WIDTH)


def rows_to_eight(x):
    return jnp.sum(x.reshape(-1, 8, WIDTH), axis=0)


def head_rows(i, g, h):
    return pl.ds(i * HALF * HEADS + GROUP * g + h, HALF, stride=HEADS)


def swap_rows(x):
    return jnp.concatenate([x[WIDTH // 2 :], x[: WIDTH // 2]], axis=0)


def mean_rows(x):
    return jnp.sum(x, axis=0, keepdims=True) * (1.0 / WIDTH)


def pack_kernel(k_hbm, v_hbm, kv_hbm, *rest):
    targets, (k_ref, v_ref, flat, kv_ref, in_sem, out_sem) = rest[:-6], rest[-6:]
    loads = [
        pltpu.make_async_copy(k_hbm, k_ref, in_sem.at[0]),
        pltpu.make_async_copy(v_hbm, v_ref, in_sem.at[1]),
    ]
    for load in loads:
        load.start()
    for n, ref in enumerate((k_ref, v_ref)):
        loads[n].wait()
        flat[...] = ref[...].astype(F32).reshape(flat.shape)
        for g in range(KV):
            kv_ref[n * KV + g] = flat[pl.ds(g, LOCAL, stride=KV), :].astype(BF16)
    stores = [pltpu.make_async_copy(kv_ref, kv_hbm, out_sem.at[0])]
    for b, target in enumerate(targets):
        size = target.shape[1]
        stores.append(
            pltpu.make_async_copy(kv_ref.at[:, pl.ds(b * size, size), :], target, out_sem.at[1 + b])
        )
    for store in stores:
        store.start()
    for store in stores:
        store.wait()


def load_all(pairs, sems):
    loads = [pltpu.make_async_copy(a, b, sems.at[n]) for n, (a, b) in enumerate(pairs)]
    for load in loads:
        load.start()
    for load in loads:
        load.wait()


def prepare_kernel(
    place_ref, rewards_ref, seg_ref, gain_ref, cos_hbm, sin_hbm, q_hbm, up_hbm, k_hbm,
    query_hbm, query_t_hbm, grad_hbm, grad_t_hbm, unit_hbm, factor_hbm, angle_hbm, own_hbm, xq, xu,
    query_ref, query_t_ref, grad_ref, grad_t_ref, unit_ref, factor_ref, angle_ref, own_ref,
    cos_ref, sin_ref, q_ref, up_ref, k_ref, in_sem, out_sem,
):
    load_all(
        [(q_hbm, q_ref), (up_hbm, up_ref), (cos_hbm, cos_ref), (sin_hbm, sin_ref), (k_hbm.at[pl.ds(0, KV)], k_ref)],
        in_sem,
    )
    xq[...] = q_ref[...].astype(F32).reshape(xq.shape)
    xu[...] = up_ref[...].astype(F32).reshape(xu.shape)
    gain = gain_ref[...]
    reward = [rewards_ref[r] for r in range(RESPONSES)]
    centre = (reward[0] + reward[1] + reward[2] + reward[3] + reward[4]) * (1.0 / RESPONSES)
    seg = seg_ref[...]
    adv_row = jnp.zeros(seg.shape, F32)
    for r in range(RESPONSES):
        adv_row = adv_row + jnp.where(seg == r + 1, reward[r] - centre, 0.0)
    for i in range(BLOCKS):
        block = BLOCKS * lax.axis_index("seq") + i
        start = place_ref[block // 2] * TILE + lax.rem(block, 2) * HALF
        start = pl.multiple_of(start, HALF)
        for n, ref in enumerate((cos_ref, sin_ref)):
            angle = ref[pl.ds(start, HALF), :]
            angle_ref[n, :, i * COLS : (i + 1) * COLS] = jnp.concatenate([angle] * GROUP, axis=0).T
            own_ref[n, i * HALF : (i + 1) * HALF, :] = angle
    for g in range(KV):
        x = k_ref[g].astype(F32)
        factor = lax.rsqrt(mean_lanes(x * x) + EPS)
        own_ref[2 + g] = x * factor
        own_ref[2 + KV + g] = jnp.broadcast_to(factor, (LOCAL, WIDTH))

    def per_kv(g, carry):
        for i in range(BLOCKS):
            span = slice(i * COLS, (i + 1) * COLS)

            def columns(ref):
                rows = [ref[head_rows(i, g, h), :] for h in range(GROUP)]
                return jnp.concatenate(rows, axis=0).T

            x = columns(xq)
            factor = lax.rsqrt(mean_rows(x * x) + EPS)
            unit = x * factor
            normed = unit * gain
            turned = normed * angle_ref[0, :, span] + swap_rows(normed) * angle_ref[1, :, span]
            query_ref[g, span, :] = turned.T.astype(BF16)
            query_t_ref[g, :, span] = turned.astype(BF16)
            unit_ref[g, :, span] = unit
            factor_ref[g, :, span] = jnp.broadcast_to(factor, (8, COLS))
            adv = jnp.concatenate([adv_row[:, i * HALF : (i + 1) * HALF]] * GROUP, axis=1)
            grad = columns(xu) * adv
            grad_t_ref[g, :, span] = grad.astype(BF16)
            grad_ref[g, span, :] = grad.T.astype(BF16)
        return carry

    lax.fori_loop(0, KV, per_kv, 0)
    stores = [
        pltpu.make_async_copy(source, target, out_sem.at[n])
        for n, (source, target) in enumerate(
            [
                (query_ref, query_hbm), (query_t_ref, query_t_hbm), (grad_ref, grad_hbm),
                (grad_t_ref, grad_t_hbm), (unit_ref, unit_hbm), (factor_ref, factor_hbm),
                (angle_ref, angle_hbm), (own_ref, own_hbm),
            ]
        )
    ]
    for store in stores:
        store.start()
    for store in stores:
        store.wait()


def attention_kernel(
    tile_count, table_ref, place_ref, gain_ref, cos_hbm, sin_hbm,
    query_hbm, query_t_hbm, grad_hbm, grad_t_hbm, unit_hbm, angle_hbm,
    parts_hbm, others_hbm, mine_hbm, hop_in_hbm, swap_in_hbm,
    out_hbm, dq_hbm, gain_out_ref, keep_hbm, send_hbm, swap_hbm, hop_hbm, own_hbm,
    out_ref, dq_ref, cos_ref, sin_ref, query_v, query_t_v, grad_v, grad_t_v, unit_v, angle_v,
    kvb, ybuf, kr, kt, vr, vt, kcos, ksin, ebuf, pbuf, dsbuf, limits, ksum, lsum, qsum,
    in_sem, out_sem,
):
    me = lax.axis_index("seq")
    wb = jnp.clip((BLOCKS * me) // 2 - 3, PROMPT, tile_count - WINDOW)
    prompt_rows = PROMPT * TILE

    def rows_of(back, skip=0):
        return pl.multiple_of((me - back) * LOCAL + skip - wb * TILE + 2 * prompt_rows, HALF)

    kvb[:, 2 * prompt_rows :, :] = jnp.zeros((PAIR, WINDOW * TILE, WIDTH), BF16)
    chips, _, share_rows, _ = parts_hbm.shape
    devices = 2 * chips
    parity = lax.rem(me, 2)
    key_loads = []
    for n in range(chips):
        for at, half, source in ((2 * n, parity, parts_hbm), (2 * n + 1, 1 - parity, others_hbm)):
            start = pl.multiple_of(half * (prompt_rows // 2) + n * share_rows, share_rows)
            target = kvb.at[:, pl.ds(start, share_rows), :]
            key_loads.append(pltpu.make_async_copy(source.at[n], target, in_sem.at[8 + at]))
    key_loads.append(pltpu.make_async_copy(cos_hbm, cos_ref, in_sem.at[6]))
    key_loads.append(pltpu.make_async_copy(sin_hbm, sin_ref, in_sem.at[7]))
    window_loads = [
        (0, pltpu.make_async_copy(mine_hbm, kvb.at[:, pl.ds(rows_of(0), LOCAL), :], in_sem.at[8 + devices]))
    ]

    def earlier(back, source, skip, size):
        start = jnp.maximum(rows_of(back, skip), prompt_rows)
        target = kvb.at[:, pl.ds(pl.multiple_of(start, HALF), size), :]
        window_loads.append((back, pltpu.make_async_copy(source, target, in_sem.at[8 + devices + back])))

    earlier(1, swap_in_hbm.at[:, pl.ds(0, LOCAL), :], 0, LOCAL)
    earlier(2, hop_in_hbm, 0, LOCAL)
    earlier(3, swap_in_hbm.at[:, pl.ds(LOCAL, HALF), :], LOCAL - HALF, HALF)
    loads = [
        pltpu.make_async_copy(query_t_hbm, query_t_v, in_sem.at[0]),
        pltpu.make_async_copy(grad_t_hbm, grad_t_v, in_sem.at[1]),
        pltpu.make_async_copy(query_hbm, query_v, in_sem.at[2]),
        pltpu.make_async_copy(grad_hbm, grad_v, in_sem.at[3]),
        pltpu.make_async_copy(unit_hbm, unit_v, in_sem.at[4]),
        pltpu.make_async_copy(angle_hbm, angle_v, in_sem.at[5]),
    ]
    for load in key_loads:
        load.start()
    for back, load in window_loads:
        pl.when(me >= back)(load.start)

    gain = gain_ref[...]
    gain_turned = swap_halves(gain)
    ksum[...] = jnp.zeros_like(ksum)
    lsum[...] = jnp.zeros_like(lsum)
    qsum[...] = jnp.zeros_like(qsum)
    ybuf[:, prompt_rows : 2 * prompt_rows] = jnp.zeros((PAIR, prompt_rows, WIDTH), BF16)

    lane = lax.broadcasted_iota(jnp.int32, (1, COLS), 1)
    key_place = [tile * TILE for tile in range(PROMPT)]
    key_place += [pl.multiple_of(place_ref[wb + j] * TILE, TILE) for j in range(WINDOW)]
    for tile in range(SPAN):
        name = tile if tile < PROMPT else wb + tile - PROMPT
        for i in range(BLOCKS):
            block = BLOCKS * me + i
            kind = table_ref[(block // 2) * tile_count + name]
            one = (kind == 1).astype(jnp.int32)
            two = (kind == 2).astype(jnp.int32)
            slot = lax.rem(block, 2) * HALF + lax.rem(lane, HALF)
            limits[tile : tile + 1, i * COLS : (i + 1) * COLS] = (
                two * slot + (one * (TILE + 1) - 1 + two)
            )

    for load in key_loads:
        load.wait()
    for back, load in window_loads:
        pl.when(me >= back)(load.wait)
    for load in loads:
        load.start()

    def prepare_keys(g, carry):
        for tile in range(SPAN):
            at = slice(tile * TILE, (tile + 1) * TILE)
            source = tile * TILE if tile < PROMPT else tile * TILE + prompt_rows
            source = slice(source, source + TILE)
            x = kvb[g, source, :].astype(F32)
            factor = lax.rsqrt(mean_lanes(x * x) + EPS)
            unit = x * factor
            first = unit * cos_ref[pl.ds(key_place[tile], TILE), :]
            second = swap_halves(unit) * sin_ref[pl.ds(key_place[tile], TILE), :]
            turned = first * gain + second * gain_turned
            kcos[g, at, :] = first
            ksin[g, at, :] = second
            kr[g, at, :] = turned.astype(BF16)
            kt[g, :, at] = turned.T.astype(BF16)
            value = kvb[KV + g, source, :]
            vr[g, at, :] = value
            vt[g, :, at] = value.astype(F32).T.astype(BF16)
        return carry

    lax.fori_loop(0, KV, prepare_keys, 0)
    for load in loads:
        load.wait()

    scale = 1.0 / math.sqrt(WIDTH)
    key_at = lax.broadcasted_iota(jnp.int32, (TILE, ALL), 0)
    third = SPAN // 3

    def per_kv(g, carry):
        query_t = query_t_v[g]
        grad_t = grad_t_v[g]
        total = jnp.zeros((1, ALL), F32)
        for c in range(3):
            rows = slice(c * third * TILE, (c + 1) * third * TILE)
            score = jnp.dot(kr[g, rows, :], query_t, preferred_element_type=F32)
            for t in range(third):
                tile = c * third + t
                raw = jnp.where(
                    key_at <= limits[tile : tile + 1, :],
                    jnp.exp2(score[t * TILE : (t + 1) * TILE] * (scale * math.log2(math.e))),
                    0.0,
                )
                ebuf[tile * TILE : (tile + 1) * TILE, :] = raw
                total = total + jnp.sum(raw, axis=0, keepdims=True)
        share = jnp.where(total > 0, 1.0 / total, 0.0)
        for tile in range(SPAN):
            at = slice(tile * TILE, (tile + 1) * TILE)
            pbuf[at, :] = (ebuf[at, :] * share).astype(BF16)
        out_t = jnp.dot(vt[g], pbuf[...], preferred_element_type=F32)
        out_ref[g] = out_t.astype(BF16)
        delta = jnp.sum(grad_t.astype(F32) * out_t, axis=0, keepdims=True)
        for c in range(3):
            rows = slice(c * third * TILE, (c + 1) * third * TILE)
            dweights = jnp.dot(vr[g, rows, :], grad_t, preferred_element_type=F32)
            dsbuf[rows, :] = (
                pbuf[rows, :].astype(F32) * (dweights - delta)
            ).astype(BF16)
        dv = jnp.dot(pbuf[...], grad_v[g], preferred_element_type=F32)
        dq_t = jnp.dot(kt[g], dsbuf[...], preferred_element_type=F32)
        dq_t = (dq_t * scale).astype(BF16)
        dq_ref[g] = dq_t
        dq_t = dq_t.astype(F32)
        dnormed = (dq_t * angle_v[0] - swap_rows(dq_t) * angle_v[1]) * unit_v[g]
        for n in range(ALL // WIDTH):
            qsum[...] += dnormed[:, n * WIDTH : (n + 1) * WIDTH]
        dk = jnp.dot(dsbuf[...], query_v[g], preferred_element_type=F32) * scale
        ksum[...] += rows_to_eight(dk * kcos[g])
        lsum[...] += rows_to_eight(dk * ksin[g])
        for at, item in ((g, dk), (KV + g, dv)):
            item = item.astype(BF16)
            ybuf[at, :prompt_rows, :] = item[:prompt_rows]
            ybuf[at, 2 * prompt_rows :, :] = item[prompt_rows:]
        pltpu.make_async_copy(out_ref.at[g], out_hbm.at[g], out_sem.at[g]).start()
        pltpu.make_async_copy(dq_ref.at[g], dq_hbm.at[g], out_sem.at[KV + g]).start()
        return carry

    lax.fori_loop(0, KV, per_kv, 0)

    def mine(back, skip=0):
        return pl.multiple_of(jnp.maximum(rows_of(back, skip), prompt_rows), HALF)

    stores = []
    for n in range(chips):
        for half, target in ((parity, keep_hbm), (1 - parity, send_hbm)):
            start = pl.multiple_of(half * (prompt_rows // 2) + n * share_rows, share_rows)
            stores.append((start, share_rows, target.at[n]))
    stores += [
        (mine(1), LOCAL, swap_hbm.at[:, pl.ds(0, LOCAL), :]),
        (mine(3, LOCAL - HALF), HALF, swap_hbm.at[:, pl.ds(LOCAL, HALF), :]),
        (mine(2), LOCAL, hop_hbm),
        (mine(0), LOCAL, own_hbm),
    ]
    stores = [
        pltpu.make_async_copy(ybuf.at[:, pl.ds(start, size), :], target, out_sem.at[PAIR + n])
        for n, (start, size, target) in enumerate(stores)
    ]
    for store in stores:
        store.start()
    gain_out_ref[0:1, :] = jnp.sum(qsum[...].T, axis=0, keepdims=True)
    second = swap_halves(jnp.sum(lsum[...], axis=0, keepdims=True))
    gain_out_ref[1:2, :] = jnp.sum(ksum[...], axis=0, keepdims=True) + second
    for g in range(KV):
        pltpu.make_async_copy(out_ref.at[g], out_hbm.at[g], out_sem.at[g]).wait()
        pltpu.make_async_copy(dq_ref.at[g], dq_hbm.at[g], out_sem.at[KV + g]).wait()
    for store in stores:
        store.wait()


def finish_kernel(
    gain_ref, angle_hbm, out_t_hbm, dq_t_hbm, unit_hbm, factor_hbm, out_ref, dq_ref, os_, dqs,
    angle_ref, out_t_ref, dq_t_ref, unit_ref, factor_ref, in_sem,
):
    pairs = [(out_t_hbm, out_t_ref), (dq_t_hbm, dq_t_ref), (unit_hbm, unit_ref), (factor_hbm, factor_ref)]

    def load(n, g):
        source, target = pairs[n]
        return pltpu.make_async_copy(source.at[g], target.at[g], in_sem.at[1 + n * KV + g])

    angles = pltpu.make_async_copy(angle_hbm, angle_ref, in_sem.at[0])
    angles.start()
    for g in range(KV):
        for n in range(len(pairs)):
            load(n, g).start()
    angles.wait()
    gain = gain_ref[...]

    def per_kv(g, carry):
        for n in range(len(pairs)):
            load(n, g).wait()
        for i in range(BLOCKS):
            span = slice(i * COLS, (i + 1) * COLS)
            out = out_t_ref[g, :, span].astype(F32).T
            dturned = dq_t_ref[g, :, span].astype(F32)
            dnormed = dturned * angle_ref[0, :, span] - swap_rows(dturned) * angle_ref[1, :, span]
            unit = unit_ref[g, :, span]
            dunit = dnormed * gain
            dx = (factor_ref[g, 0:1, span] * (dunit - unit * mean_rows(dunit * unit))).T
            for h in range(GROUP):
                os_[head_rows(i, g, h), :] = out[h * HALF : (h + 1) * HALF]
                dqs[head_rows(i, g, h), :] = dx[h * HALF : (h + 1) * HALF]
        return carry

    lax.fori_loop(0, KV, per_kv, 0)
    out_ref[...] = os_[...].reshape(out_ref.shape).astype(BF16)
    dq_ref[...] = dqs[...].reshape(dq_ref.shape).astype(BF16)


def last_kernel(
    gain_ref, key_ref, own_ref, swap_ref, back_ref, *rest,
):
    blocks, (dk_ref, dv_ref, flat) = rest[:-3], rest[-3:]
    gain = gain_ref[...]
    even = (1 - lax.rem(lax.axis_index("seq"), 2)).astype(F32)

    for ref, first in ((dk_ref, 0), (dv_ref, KV)):
        for g in range(KV):
            at = first + g
            prompt = jnp.concatenate([block[at] for block in blocks], axis=0).astype(F32)
            summed = own_ref[at].astype(F32) + back_ref[at].astype(F32) + prompt
            summed = summed + even * swap_ref[at, :LOCAL].astype(F32)
            if first == 0:
                dnormed = summed * key_ref[0] - swap_halves(summed) * key_ref[1]
                unit = key_ref[2 + g]
                dunit = dnormed * gain
                summed = key_ref[2 + KV + g] * (dunit - unit * mean_lanes(dunit * unit))
            flat[pl.ds(g, LOCAL, stride=KV), :] = summed
        ref[...] = flat[...].reshape(ref.shape).astype(BF16)


def shape(dims, dtype=BF16):
    return jax.ShapeDtypeStruct(dims, dtype)


def cost(flops, size):
    return pl.CostEstimate(flops=flops, bytes_accessed=size, transcendentals=0)


def params(mib):
    return pltpu.CompilerParams(vmem_limit_bytes=mib * 1024 * 1024)


def pack(k, v, share):
    blocks = LOCAL // share
    return pl.pallas_call(
        pack_kernel,
        out_shape=[shape((PAIR, LOCAL, WIDTH))] + [shape((PAIR, share, WIDTH))] * blocks,
        in_specs=[HBM] * 2,
        out_specs=[HBM] * (1 + blocks),
        scratch_shapes=[
            pltpu.VMEM(k.shape, BF16), pltpu.VMEM(k.shape, BF16), pltpu.VMEM((LOCAL * KV, WIDTH), F32),
            pltpu.VMEM((PAIR, LOCAL, WIDTH), BF16),
            pltpu.SemaphoreType.DMA((2,)), pltpu.SemaphoreType.DMA((1 + blocks,)),
        ],
        compiler_params=params(56),
        cost_estimate=cost(1_000_000, 2_000_000),
        name="pack_keys",
    )(k, v)


def prepare(place, rewards, seg, gain, cosine, sine, q, up, k):
    rows = (KV, ALL, WIDTH)
    cols = (KV, WIDTH, ALL)
    shapes = [
        (rows, BF16), (cols, BF16), (rows, BF16), (cols, BF16), (cols, F32), ((KV, 8, ALL), F32),
        ((2, WIDTH, ALL), F32), ((2 + PAIR, LOCAL, WIDTH), F32),
    ]
    return pl.pallas_call(
        prepare_kernel,
        out_shape=[shape(*item) for item in shapes],
        in_specs=[SMEM, SMEM, VMEM, VMEM] + [HBM] * 5,
        out_specs=[HBM] * 8,
        scratch_shapes=[pltpu.VMEM((LOCAL * HEADS, WIDTH), F32)] * 2
        + [pltpu.VMEM(*item) for item in shapes]
        + [pltpu.VMEM(item.shape, item.dtype) for item in (cosine, sine, q, up)]
        + [pltpu.VMEM((KV, LOCAL, WIDTH), BF16), pltpu.SemaphoreType.DMA((5,)), pltpu.SemaphoreType.DMA((8,))],
        compiler_params=params(56),
        cost_estimate=cost(100_000_000, 16_000_000),
        name="prepare_queries",
    )(place, rewards, seg, gain, cosine, sine, q, up, k)


def attend(table, place, gain, cosine, sine, *operands):
    angle, parts = operands[5:7]
    devices, share = 2 * parts.shape[0], parts.shape[2]
    tile_count = devices * LOCAL // TILE
    span_rows = SPAN * TILE
    rows = (KV, ALL, WIDTH)
    cols = (KV, WIDTH, ALL)
    keys = (KV, span_rows, WIDTH)
    keys_t = (KV, WIDTH, span_rows)
    return pl.pallas_call(
        functools.partial(attention_kernel, tile_count),
        out_shape=(
            shape(cols), shape(cols), shape((2, WIDTH), F32),
            shape((devices // 2, PAIR, share, WIDTH)), shape((devices // 2, PAIR, share, WIDTH)),
            shape((PAIR, LOCAL + HALF, WIDTH)), shape((PAIR, LOCAL, WIDTH)), shape((PAIR, LOCAL, WIDTH)),
        ),
        in_specs=[SMEM, SMEM, VMEM] + [HBM] * 13,
        out_specs=(HBM, HBM, VMEM) + (HBM,) * 5,
        scratch_shapes=[
            pltpu.VMEM(cols, BF16), pltpu.VMEM(cols, BF16),
            pltpu.VMEM(cosine.shape, F32), pltpu.VMEM(cosine.shape, F32),
            pltpu.VMEM(rows, BF16), pltpu.VMEM(cols, BF16), pltpu.VMEM(rows, BF16), pltpu.VMEM(cols, BF16),
            pltpu.VMEM(cols, F32), pltpu.VMEM(angle.shape, F32),
            pltpu.VMEM((PAIR, span_rows + PROMPT * TILE, WIDTH), BF16),
            pltpu.VMEM((PAIR, span_rows + PROMPT * TILE, WIDTH), BF16),
            pltpu.VMEM(keys, BF16), pltpu.VMEM(keys_t, BF16), pltpu.VMEM(keys, BF16), pltpu.VMEM(keys_t, BF16),
            pltpu.VMEM(keys, F32), pltpu.VMEM(keys, F32),
            pltpu.VMEM((span_rows, ALL), F32),
            pltpu.VMEM((span_rows, ALL), BF16), pltpu.VMEM((span_rows, ALL), BF16),
            pltpu.VMEM((16, ALL), jnp.int32),
            pltpu.VMEM((8, WIDTH), F32), pltpu.VMEM((8, WIDTH), F32), pltpu.VMEM((WIDTH, WIDTH), F32),
            pltpu.SemaphoreType.DMA((12 + devices,)), pltpu.SemaphoreType.DMA((devices + 4 + PAIR,)),
        ],
        compiler_params=params(56),
        cost_estimate=cost(12 * span_rows * ALL * WIDTH * KV, 12_000_000),
        name="tree_attention",
    )(table, place, gain, cosine, sine, *operands)


def finish(gain, angle, out_t, dq_t, unit, factor):
    dims = (LOCAL, HEADS, WIDTH)
    return pl.pallas_call(
        finish_kernel,
        out_shape=(shape(dims), shape(dims)),
        in_specs=[VMEM] + [HBM] * 5,
        out_specs=(VMEM,) * 2,
        scratch_shapes=[pltpu.VMEM((LOCAL * HEADS, WIDTH), F32)] * 2
        + [pltpu.VMEM(item.shape, item.dtype) for item in (angle, out_t, dq_t, unit, factor)]
        + [pltpu.SemaphoreType.DMA((1 + 4 * KV,))],
        compiler_params=params(56),
        cost_estimate=cost(100_000_000, 10_000_000),
        name="finish_queries",
    )(gain, angle, out_t, dq_t, unit, factor)


def last(gain, key, own, swap, back, blocks):
    dims = (LOCAL, KV, WIDTH)
    return pl.pallas_call(
        last_kernel,
        out_shape=(shape(dims), shape(dims)),
        in_specs=[VMEM] * (5 + len(blocks)),
        out_specs=(VMEM,) * 2,
        scratch_shapes=[pltpu.VMEM((LOCAL * KV, WIDTH), F32)],
        compiler_params=params(24),
        cost_estimate=cost(1_000_000, 4_000_000),
        name="finish_keys",
    )(gain, key, own, swap, back, *blocks)


def tile_table(tiles, count):
    ids = jnp.arange(count, dtype=jnp.int32)
    row_hits = (tiles[:, 0, None] == ids).astype(jnp.int32) * tiles[:, 2, None]
    col_hits = (tiles[:, 1, None] == ids).astype(jnp.int32)
    table = jnp.einsum("tq,tk->qk", row_hits, col_hits)
    live = (table > 0) & (ids[None, :] >= PROMPT)
    first = jnp.min(jnp.where(live, ids[None, :], count), axis=1)
    inside = (ids >= PROMPT) & (first < count)
    place = jnp.minimum(jnp.where(inside, PROMPT + ids - first, ids), 2 * PROMPT - 1)
    return table.reshape(-1), place


def sum_four(x, axis, step):
    size = lax.axis_size(axis)
    if size <= step:
        return x
    a, b, c = (
        lax.ppermute(x, axis, [(i, i ^ (n * step)) for i in range(size)]) for n in (1, 2, 3)
    )
    return (x + a) + (b + c)


def prompt_pairs(devices, per_owner):
    routes = []
    chips = devices // 2
    for b in range(per_owner):
        pairs = [(owner, owner * per_owner + b) for owner in range(3)]
        routes.append([(owner, 2 * (p % chips) + p // chips) for owner, p in pairs if p < devices])
    return routes


def per_device(q_proj, k_proj, v_proj, upstream, segment_ids, tree_tiles, rewards, q_gain, k_gain):
    devices = lax.axis_size("seq")
    share = PROMPT * TILE // devices
    tile_count = devices * LOCAL // TILE
    routes = prompt_pairs(devices, LOCAL // share)
    even = lax.rem(lax.axis_index("seq"), 2) == 0
    cores = [(i, i ^ 1) for i in range(devices)]

    kv, *blocks = pack(k_proj[0], v_proj[0], share)
    mine = [lax.ppermute(block, "seq", pairs) for block, pairs in zip(blocks, routes)]
    hop_in = lax.ppermute(kv, "seq", [(i, i + 2) for i in range(devices - 2)])
    mine = mine[0] + mine[1] + mine[2] + mine[3] + mine[4] + mine[5]
    mine, hop_in = lax.optimization_barrier((mine, hop_in))
    chips = devices // 2
    parities = [list(range(j, devices, 2)) for j in range(2)]

    def exchange(x):
        return lax.all_to_all(x, "seq", split_axis=0, concat_axis=0, tiled=True, axis_index_groups=parities)

    parts = exchange(jnp.broadcast_to(mine[None], (chips,) + mine.shape))
    swap_in = jnp.where(
        even,
        jnp.concatenate([kv, hop_in[:, LOCAL - HALF :]], axis=1),
        jnp.concatenate([hop_in, hop_in[:, LOCAL - HALF :]], axis=1),
    )
    swap_in = lax.ppermute(swap_in, "seq", cores)

    table, place = tile_table(tree_tiles[0], tile_count)
    cosine, sine = (jnp.asarray(item) for item in rope_tables(2 * PROMPT * TILE))
    query, query_t, grad, grad_t, unit, factor, angle, own_key = prepare(
        place, rewards[0], segment_ids, q_gain[:, None], cosine, sine, q_proj[0], upstream[0],
        kv,
    )
    parts, swap_in, query = lax.optimization_barrier((parts, swap_in, query))
    others = lax.ppermute(parts, "seq", cores)
    out_t, dq_t, gains, keep, send, swap, hop, own = attend(
        table, place, k_gain[None], cosine, sine, query, query_t, grad, grad_t, unit, angle,
        parts, others, kv, hop_in, swap_in,
    )

    got = lax.ppermute(send, "seq", cores)
    parts = exchange(keep + got)
    swap = lax.ppermute(swap, "seq", cores)
    far = jnp.concatenate([jnp.zeros((PAIR, LOCAL - HALF, WIDTH), BF16), swap[:, LOCAL:]], axis=1)
    hop = hop + jnp.where(even, far, swap[:, :LOCAL])
    back = lax.ppermute(hop, "seq", [(i, i - 2) for i in range(2, devices)])
    gains = sum_four(gains, "dp", 1)
    gains, out_t, dq_t = lax.optimization_barrier((gains, out_t, dq_t))
    out, dq = finish(q_gain[:, None], angle, out_t, dq_t, unit, factor)
    gains = sum_four(sum_four(gains, "dp", 4), "seq", 4)
    piece = jnp.sum(parts.astype(F32), axis=0).astype(BF16)
    piece, gains, out, dq = lax.optimization_barrier((piece, gains, out, dq))
    blocks = [lax.ppermute(piece, "seq", [(b, a) for a, b in pairs]) for pairs in routes]
    gains = sum_four(gains, "seq", 1)
    dk, dv = last(k_gain[None], own_key, own, swap, back, blocks)
    return (out[None], dq[None], dk[None], dv[None], gains[0], gains[1])


def solution(mesh):
    whole = P("dp", "seq", None, None)
    return jax.shard_map(
        per_device,
        mesh=mesh,
        in_specs=(whole, whole, whole, whole, P("dp", "seq"), P("dp", None, None), P("dp", None), P(), P()),
        out_specs=(whole, whole, whole, whole, P(), P()),
        check_vma=False,
    )
```
